1024 devices in a mesh: dp: 8 (over x, core), ep: 32 (over z, y_hi), tp: 4 (over y_lo).
Axes of the slice: x: 4, y: 8 (y_hi: 2, y_lo: 4; y = y_hi * 4 + y_lo), z: 16, core: 2. Of those that a mesh axis runs over, the one named last changes fastest.
Arguments:
- tokens: bfloat16 [32768, 4096], P(('dp', 'ep'), 'tp'), may hold values from -6 to 6
- expert_ids: int32 [32768, 8], P(('dp', 'ep')), may hold values from 0 to 127, all different within a row; in each aligned block of 128 rows (0 to 127, 128 to 255, ...) at most 10 rows name the same one
- route_weight: float32 [32768, 8], P(('dp', 'ep')), may hold values from 0.05 to 0.5
- gate_up: bfloat16 [32, 2, 1536, 4096], P('ep', None, None, 'tp'), may hold values from -0.09375 to 0.09375
- down_proj: bfloat16 [32, 1536, 4096], P('ep', None, 'tp'), may hold values from -0.15625 to 0.15625
Outputs:
- mixed: bfloat16 [32768, 4096], P(('dp', 'ep'), 'tp')
The draws below stay inside these ranges and needn't reach their ends.
Inputs may be any that keep to these rules, and one draw needn't show every extreme that they name: `expert_ids`: each row names 8 different experts. Among the 128 rows of one block no expert is named more than 10 times, and in some block one expert is named exactly 10 times.
All inputs are finite; a program needn't handle non-finite values.
Results may differ from the reference program's by a relative error of at most 0.024.
Values may be sent and summed in bfloat16 or wider, within the bound.
No kernel may reach another device: no remote copies, remote signals or barrier semaphores. Data moves between devices by JAX's collectives and lax.ppermute only.
A program may use at most 32 MiB of HBM per device.

```python
import math
import jax
import jax.numpy as jnp
import numpy as np
from jax import lax

D = 4096
EXPERTS = 128
TOP = 8
FF = 1536
TOK_DEV = 128
CAP = 10
FLIGHT = 32
TOKENS = 32768
N_DP = 8
N_EP = 32
N_TP = 4


def block_scale(rng, dims, shards, least, largest):
    factor_of = 1.0
    for dim, parts in shards:
        steps = jax.random.uniform(jax.random.fold_in(jax.random.fold_in(rng, 6), dim), (parts,), jnp.float32, least / len(shards), largest / len(shards))
        factor_of = factor_of * jnp.repeat(jnp.exp(steps), dims[dim] // parts).reshape((-1,) + (1,) * (len(dims) - 1 - dim))
    return factor_of


def routed_block(key, own, number, rows, count, top, limit, slope):
    order = jax.random.permutation(key, count)
    crowded, ordinary = shares(count, rows * top, limit, slope, True), shares(count, rows * top, limit, slope, False)
    places = jnp.arange(count)

    def named(sizes, turn):
        used = int((sizes > 0).sum())
        fixed = max(1, used // 4)
        passed = fixed + (places - fixed + turn * (used - fixed)) % max(1, count - fixed)
        return jnp.zeros((count,), jnp.int32).at[order[jnp.where(places < fixed, places, passed)]].set(jnp.asarray(sizes, jnp.int32))

    sizes = jnp.where(number % 4 == 0, named(crowded, number // 4), named(ordinary, number - number // 4 - 1))
    mixed = jax.random.permutation(jax.random.fold_in(own, 3), count)
    donor, taker = mixed[0:count // 2 * 2:2], mixed[1:count // 2 * 2:2]
    margin = jnp.minimum(sizes[donor] - 1, limit - sizes[taker]) // 2
    margin = jnp.where((donor == order[0]) | (taker == order[0]) | (sizes[taker] == 0), 0, jnp.maximum(margin, 0))
    passed = jax.random.randint(jax.random.fold_in(own, 4), (count // 2,), 0, 1 << 20) % (margin + 1)
    sizes = sizes.at[donor].add(-passed).at[taker].add(passed)
    labels = jnp.searchsorted(jnp.cumsum(sizes), jnp.arange(rows * top), side="right").astype(jnp.int32)
    table = labels.reshape(top, rows).T
    table = table[jax.random.permutation(jax.random.fold_in(own, 1), rows)]
    turn = jax.random.randint(jax.random.fold_in(own, 2), (rows, 1), 0, top)
    return jnp.take_along_axis(table, (jnp.arange(top)[None, :] + turn) % top, axis=1)


def shares(count, total, bound, skew, full):
    weights = [(1 << 20) // math.isqrt(grade ** skew) + 1 for grade in range(1, count + 1)]
    largest = bound if full else min(bound, max(-(-total // count), total * weights[0] // sum(weights)))
    least = 1 if total - largest >= count - 1 else 0
    given, spare = [largest] + [least] * (count - 1), total - largest - least * (count - 1)
    while spare > 0:
        free = [i for i in range(1, count) if given[i] < largest] or [i for i in range(1, count) if given[i] < bound]
        whole, budget = sum([weights[i] for i in free]), spare
        for i in free:
            extra = min(bound - given[i], max(1, budget * weights[i] // whole), spare)
            given[i] = given[i] + extra
            spare = spare - extra
    return np.array(given)


def scatter_about(rng, shape, deviation, limit, cuts=(), kind=jnp.bfloat16):
    values = deviation * jax.random.normal(rng, shape, jnp.float32)
    if cuts:
        values = values * block_scale(rng, shape, cuts, -0.22, 0.18)
    return jnp.clip(values, -limit, limit).astype(kind)


def setup_inputs(seed: int = 0) -> dict:
    arg_keys = jax.random.split(jax.random.key(seed), 6)
    tokens = scatter_about(arg_keys[0], (TOKENS, D), 1.0, 6.0, ((0, 256), (1, 4)))
    expert_ids_keys = jax.random.split(jax.random.fold_in(arg_keys[1], 1), TOKENS // TOK_DEV)
    expert_ids_turns = jax.random.permutation(jax.random.fold_in(arg_keys[1], 3), TOKENS // TOK_DEV)
    expert_ids = jax.vmap(lambda own, number: routed_block(jax.random.fold_in(arg_keys[1], 2), own, number, TOK_DEV, EXPERTS, TOP, CAP, 2))(expert_ids_keys, expert_ids_turns).reshape((TOKENS, TOP))
    route_weight = jnp.clip(jnp.exp(math.log(0.5) - 2.3025851 * jax.random.uniform(arg_keys[2], (TOKENS, TOP), jnp.float32) ** block_scale(arg_keys[2], (TOKENS, TOP), ((0, 256),), -0.2, 0.2)), 0.05, 0.5)
    gate_up = scatter_about(arg_keys[3], (FLIGHT, 2, FF, D), D ** -0.5, 0.09375, ((0, 32), (3, 4)))
    down_proj = scatter_about(arg_keys[4], (FLIGHT, FF, D), FF ** -0.5, 0.15625, ((0, 32), (2, 4)))
    return dict(tokens=tokens, expert_ids=expert_ids, route_weight=route_weight, gate_up=gate_up, down_proj=down_proj)


def slot_table(routed_ids, flight, capacity):
    flat_ids = routed_ids.reshape(-1)
    matches = (flat_ids[:, None] == jnp.arange(flight, dtype=jnp.int32)[None, :]).astype(jnp.int32)
    before = jnp.cumsum(matches, axis=0) - matches
    slot_index = jnp.sum(before * matches, axis=1).astype(jnp.int32)
    placed = jnp.where(flat_ids < flight, flat_ids * capacity + slot_index, -1)
    return placed.astype(jnp.int32).reshape(routed_ids.shape)


def pack_rows(position, token_rows, places):
    target_hits = position[:, :, None] == jnp.arange(places, dtype=jnp.int32)[None, None, :]
    selector = jnp.any(target_hits, axis=1).T.astype(token_rows.dtype)
    return jnp.dot(selector, token_rows, preferred_element_type=jnp.float32).astype(jnp.bfloat16)


def expert_rows(operands):
    expert_in, weights_in, weights_out = operands
    feature_piece = D // N_TP
    preact = jnp.zeros((expert_in.shape[0], 2, FF), jnp.float32)
    for index in range(N_TP):
        start = index * feature_piece
        stop = start + feature_piece
        section = expert_in[:, start:stop]
        gate_part = jnp.dot(section, weights_in[0, :, start:stop].T, preferred_element_type=jnp.float32)
        up_part = jnp.dot(section, weights_in[1, :, start:stop].T, preferred_element_type=jnp.float32)
        partial_value = jnp.stack([gate_part, up_part], axis=1).astype(jnp.bfloat16)
        partial_value = lax.optimization_barrier(partial_value)
        preact = preact + partial_value.astype(jnp.float32)
    hidden = (jax.nn.silu(preact[:, 0]) * preact[:, 1]).astype(jnp.bfloat16)
    return jnp.dot(hidden, weights_out, preferred_element_type=jnp.float32).astype(jnp.bfloat16)


def combine(position, weight, returned):
    picked = returned[jnp.maximum(position, 0)].astype(jnp.float32)
    coefficient = jnp.where(position >= 0, weight, 0.0).astype(jnp.float32)
    return jnp.sum(coefficient[:, :, None] * picked, axis=1).astype(jnp.bfloat16)


def reference(tokens, expert_ids, route_weight, gate_up, down_proj):
    flight = N_EP
    places = flight * CAP
    all_ids = expert_ids.reshape(N_DP, N_EP, TOK_DEV, TOP)
    all_rows = tokens.reshape(N_DP, N_EP, TOK_DEV, D)
    all_weight = route_weight.reshape(N_DP, N_EP, TOK_DEV, TOP)

    def one_group(operands):
        group_ids, group_rows, group_weight = operands
        positions = lax.map(lambda routed: slot_table(routed, flight, CAP), group_ids)

        def pack_one(pair):
            return pack_rows(pair[0], pair[1], places)

        sent = lax.map(pack_one, (positions, group_rows))
        by_expert = sent.reshape(N_EP, flight, CAP, D).transpose(1, 0, 2, 3).reshape(flight, N_EP * CAP, D)
        outputs = lax.map(expert_rows, (by_expert, gate_up, down_proj))
        returned = outputs.reshape(flight, N_EP, CAP, D).transpose(1, 0, 2, 3).reshape(N_EP, places, D)

        def combine_one(triple):
            return combine(triple[0], triple[1], triple[2])

        return lax.map(combine_one, (positions, group_weight, returned))

    mixed = lax.map(one_group, (all_ids, all_rows, all_weight))
    return mixed.reshape(TOKENS, D)
```

```python
import jax
import jax.numpy as jnp
import numpy as np
from jax import lax
from jax.experimental import pallas as pl
from jax.experimental.pallas import tpu as pltpu
from jax.sharding import PartitionSpec as P

CAP = 10
QUARTERS = 4
FAR = 200.0
APART = 512.0
BF16 = jnp.bfloat16
F32 = jnp.float32
PARAMS = pltpu.CompilerParams(vmem_limit_bytes=48 * 1024 * 1024)
BLOCK = QUARTERS * CAP
GROUP = 8


def mm(a, b):
    return jnp.dot(a, b, preferred_element_type=F32)


def mm_t(a, b):
    return lax.dot_general(a, b, (((1,), (1,)), ((), ())), preferred_element_type=F32)


def place_code(flight):
    rows = np.arange(flight * BLOCK)
    expert, quarter, slot = rows // BLOCK, rows // CAP % QUARTERS, rows % CAP
    code = np.zeros((rows.size, flight + 16), np.float32)
    code[rows, expert] = 1
    code[:, flight] = -slot
    code[rows, flight + 1 + quarter] = APART
    return code


def quarter_code(rows):
    code = np.zeros((16, QUARTERS * rows), np.float32)
    code[0] = 1
    for quarter in range(QUARTERS):
        code[1 + quarter] = np.arange(QUARTERS * rows) // rows != quarter
    return code


def regroup_code():
    source, quarter, slot = np.meshgrid(np.arange(GROUP), np.arange(QUARTERS), np.arange(CAP), indexing="ij")
    code = np.zeros((GROUP * BLOCK, GROUP * BLOCK), np.float32)
    code[(quarter * GROUP + source) * CAP + slot, (source * QUARTERS + quarter) * CAP + slot] = 1
    return code


def pack_kernel(ids_ref, token_ref, earlier_ref, place_ref, quarter_ref, out_ref):
    top, rows = ids_ref.shape
    flight = place_ref.shape[1] - 16
    cols = out_ref.shape[1]
    expert = lax.broadcasted_iota(jnp.int32, (flight, rows), 0)
    named = jnp.zeros((flight, rows), F32)
    for k in range(top):
        named += jnp.where(ids_ref[k : k + 1, :] == expert, 1.0, 0.0)
    slot = mm(named.astype(BF16), earlier_ref[...])
    slot = jnp.where(named > 0, slot, FAR).astype(BF16)
    code = jnp.concatenate([jnp.concatenate([slot] * QUARTERS, axis=1), quarter_ref[...]], axis=0)
    gap = mm(place_ref[...], code)
    selector = jnp.where(gap == 0, 1.0, 0.0).astype(BF16)
    stacked = jnp.concatenate([token_ref[:, q * cols : (q + 1) * cols] for q in range(QUARTERS)], axis=0)
    out_ref[...] = mm(selector, stacked).astype(BF16)


def pack(ids_t, tokens, flight):
    rows, features = tokens.shape
    places = flight * BLOCK
    steps = 4
    earlier = jnp.asarray(np.triu(np.ones((rows, rows), np.float32), 1), BF16)
    place = jnp.asarray(place_code(flight), BF16)
    quarter = jnp.asarray(quarter_code(rows), BF16)
    whole = lambda a: pl.BlockSpec(a.shape, lambda i: (0, 0))
    return pl.pallas_call(
        pack_kernel,
        out_shape=jax.ShapeDtypeStruct((places, features // QUARTERS), BF16),
        grid=(steps,),
        in_specs=[whole(ids_t), whole(tokens), whole(earlier),
                  pl.BlockSpec((places // steps, place.shape[1]), lambda i: (i, 0)), whole(quarter)],
        out_specs=pl.BlockSpec((places // steps, features // QUARTERS), lambda i: (i, 0)),
        compiler_params=PARAMS,
        name="pack",
    )(ids_t, tokens, earlier, place, quarter)


def first_kernel(order_ref, x_ref, regroup_ref, weight_ref, rows_ref, out_ref):
    cols = x_ref.shape[1]
    span, slab = GROUP * BLOCK, GROUP * CAP
    for g in range(x_ref.shape[0] // span):
        sorted_rows = mm(regroup_ref[...], x_ref[g * span : (g + 1) * span, :]).astype(BF16)
        for q in range(QUARTERS):
            rows_ref[g * slab : (g + 1) * slab, q * cols : (q + 1) * cols] = sorted_rows[q * slab : (q + 1) * slab]
    units = weight_ref.shape[2]
    for h in range(2):
        out_ref[:, h * units : (h + 1) * units] = mm_t(rows_ref[...], weight_ref[h, 0]).astype(BF16)


def first_part(order, received, weights):
    places, cols = received.shape
    rows = places // QUARTERS
    features = weights.shape[3]
    units = weights.shape[2]
    regroup = jnp.asarray(regroup_code(), BF16)
    whole = lambda shape: pl.BlockSpec(shape, lambda i, order: (0, 0))
    return pl.pallas_call(
        first_kernel,
        out_shape=(jax.ShapeDtypeStruct((rows, features), BF16), jax.ShapeDtypeStruct((rows, 2 * units), BF16)),
        grid_spec=pltpu.PrefetchScalarGridSpec(
            num_scalar_prefetch=1,
            grid=(1,),
            in_specs=[whole((places, cols)), whole(regroup.shape),
                      pl.BlockSpec((2, 1, units, features), lambda i, order: (0, order[i], 0, 0))],
            out_specs=(whole((rows, features)), whole((rows, 2 * units))),
        ),
        compiler_params=PARAMS,
        cost_estimate=pl.CostEstimate(flops=4 * rows * units * features, bytes_accessed=4 * units * features, transcendentals=0),
        name="first",
    )(order, received, regroup, weights)


def rest_kernel(order_ref, rows_ref, weight_ref, *out_refs):
    units = weight_ref.shape[2]
    for j, out_ref in enumerate(out_refs):
        @pl.when(pl.program_id(0) == j)
        def _():
            for h in range(2):
                out_ref[:, h * units : (h + 1) * units] = mm_t(rows_ref[...], weight_ref[h, 0]).astype(BF16)


def rest_parts(order, rows_in, weights, count):
    rows, features = rows_in.shape
    units = weights.shape[2]
    whole = lambda shape: pl.BlockSpec(shape, lambda i, order: (0, 0))
    return pl.pallas_call(
        rest_kernel,
        out_shape=(jax.ShapeDtypeStruct((rows, 2 * units), BF16),) * count,
        grid_spec=pltpu.PrefetchScalarGridSpec(
            num_scalar_prefetch=1,
            grid=(count,),
            in_specs=[whole((rows, features)),
                      pl.BlockSpec((2, 1, units, features), lambda i, order: (0, order[i], 0, 0))],
            out_specs=(whole((rows, 2 * units)),) * count,
        ),
        compiler_params=PARAMS,
        cost_estimate=pl.CostEstimate(flops=4 * count * rows * units * features, bytes_accessed=4 * count * units * features, transcendentals=0),
        name="rest",
    )(order, rows_in, weights)


def down_kernel(hidden_ref, weight_ref, spread_ref, out_ref, total):
    step = pl.program_id(0)
    cols = out_ref.shape[1]
    span, slab = GROUP * BLOCK, GROUP * CAP
    part = mm(hidden_ref[0], weight_ref[0])

    @pl.when(step == 0)
    def _():
        total[...] = part

    @pl.when(step > 0)
    def _():
        total[...] += part

    @pl.when(step == pl.num_programs(0) - 1)
    def _():
        for g in range(out_ref.shape[0] // span):
            block = total[g * slab : (g + 1) * slab, :].astype(BF16)
            stacked = jnp.concatenate([block[:, q * cols : (q + 1) * cols] for q in range(QUARTERS)], axis=0)
            out_ref[g * span : (g + 1) * span, :] = mm(spread_ref[...], stacked).astype(BF16)


def down(hidden, weights):
    parts, rows, units = hidden.shape
    features = weights.shape[2]
    cols = features // QUARTERS
    spread = jnp.asarray(regroup_code().T, BF16)
    return pl.pallas_call(
        down_kernel,
        out_shape=jax.ShapeDtypeStruct((rows * QUARTERS, cols), BF16),
        grid=(parts,),
        in_specs=[pl.BlockSpec((1, rows, units), lambda i: (i, 0, 0)),
                  pl.BlockSpec((1, units, features), lambda i: (i, 0, 0)),
                  pl.BlockSpec(spread.shape, lambda i: (0, 0))],
        out_specs=pl.BlockSpec((rows * QUARTERS, cols), lambda i: (0, 0)),
        scratch_shapes=[pltpu.VMEM((rows, features), F32)],
        compiler_params=PARAMS,
        name="down",
    )(hidden, weights, spread)


def mixer_kernel(ids_ref, weight_ref, earlier_ref, expert_ref, slot_ref, quarter_ref, out_ref):
    rows, top = ids_ref.shape
    flight = expert_ref.shape[0]
    expert = lax.broadcasted_iota(jnp.int32, (rows, flight), 1)
    named = jnp.zeros((rows, flight), F32)
    weight = jnp.zeros((rows, flight), F32)
    for k in range(top):
        hit = ids_ref[:, k : k + 1] == expert
        named += jnp.where(hit, 1.0, 0.0)
        weight += jnp.where(hit, weight_ref[:, k : k + 1], 0.0)
    slot = mm(earlier_ref[...], named.astype(BF16))
    slot = jnp.where(named > 0, slot, FAR).astype(BF16)
    gap = mm(slot, expert_ref[...]) + mm(quarter_ref[...], slot_ref[...])
    out_ref[...] = jnp.where(gap == 0, mm(weight.astype(BF16), expert_ref[...]), 0.0).astype(BF16)


def mixer(ids, weight, flight):
    rows = ids.shape[0]
    places = flight * BLOCK
    code = place_code(flight).T
    earlier = jnp.asarray(np.tril(np.ones((rows, rows), np.float32), -1), BF16)
    expert, slot = jnp.asarray(code[:flight], BF16), jnp.asarray(code[flight:], BF16)
    quarter = jnp.asarray(quarter_code(rows).T, BF16)
    whole = lambda a: pl.BlockSpec(a.shape, lambda i: (0, 0))
    return pl.pallas_call(
        mixer_kernel,
        out_shape=jax.ShapeDtypeStruct((QUARTERS * rows, places), BF16),
        grid=(QUARTERS,),
        in_specs=[whole(ids), whole(weight), whole(earlier), whole(expert), whole(slot),
                  pl.BlockSpec((rows, 16), lambda i: (i, 0))],
        out_specs=pl.BlockSpec((rows, places), lambda i: (i, 0)),
        compiler_params=PARAMS,
        name="mixer",
    )(ids, weight, earlier, expert, slot, quarter)


def combine_kernel(mixer_ref, returned_ref, out_ref):
    out_ref[...] = mm(mixer_ref[...], returned_ref[...]).astype(BF16)


def combine(mix, returned):
    places, cols = returned.shape
    rows = mix.shape[0] // QUARTERS
    return pl.pallas_call(
        combine_kernel,
        out_shape=jax.ShapeDtypeStruct((rows, QUARTERS * cols), BF16),
        grid=(QUARTERS,),
        in_specs=[pl.BlockSpec((rows, places), lambda i: (i, 0)), pl.BlockSpec((places, cols), lambda i: (0, 0))],
        out_specs=pl.BlockSpec((rows, cols), lambda i: (0, i)),
        compiler_params=PARAMS,
        name="combine",
    )(mix, returned)


def local(tokens, expert_ids, route_weight, gate_up, down_proj):
    flight = lax.axis_size("ep")
    n_tp = lax.axis_size("tp")
    features = tokens.shape[1]
    cols = features // QUARTERS
    units = gate_up.shape[2] // n_tp
    up_weights = gate_up.reshape(2, n_tp, units, features)
    down_weights = down_proj.reshape(n_tp, units, features)
    me = lax.axis_index("tp")
    order = jnp.stack([me ^ 3, me ^ 1, me ^ 2, me]).astype(jnp.int32)
    near = [(i, i ^ 1) for i in range(n_tp)]
    far = [(i, i ^ 2) for i in range(n_tp)]

    sent = pack(expert_ids.T, tokens, flight)
    received = lax.all_to_all(sent.reshape(flight, BLOCK, cols), "ep", 0, 0, tiled=True).reshape(flight * BLOCK, cols)

    row_block, for_far = first_part(order[:1], received, up_weights)
    got_far = lax.ppermute(for_far, "tp", near)
    for_near, keep_far, keep = rest_parts(order[1:], row_block, up_weights, 3)
    pair_far = (got_far.astype(F32) + keep_far.astype(F32)).astype(BF16)
    for_near, pair_far = lax.optimization_barrier((for_near, pair_far))
    got = lax.ppermute(pair_far, "tp", far)
    got_near = lax.ppermute(for_near, "tp", near)
    summed = got.astype(F32) + got_near.astype(F32) + keep.astype(F32)
    hidden = (jax.nn.silu(summed[:, :units]) * summed[:, units:]).astype(BF16)
    hidden = lax.all_gather(hidden, "tp", axis=0, tiled=False)

    result = down(hidden, down_weights)
    returned = lax.all_to_all(result.reshape(flight, BLOCK, cols), "ep", 0, 0, tiled=True).reshape(flight * BLOCK, cols)
    mix = mixer(expert_ids, route_weight, flight)
    return combine(mix, returned)


def solution(mesh):
    return jax.shard_map(
        local,
        mesh=mesh,
        in_specs=(
            P(("dp", "ep"), "tp"),
            P(("dp", "ep"), None),
            P(("dp", "ep"), None),
            P("ep", None, None, "tp"),
            P("ep", None, "tp"),
        ),
        out_specs=P(("dp", "ep"), "tp"),
        check_vma=False,
    )
```

```python
import functools

import jax
import jax.numpy as jnp
import numpy as np
from jax import lax
from jax.experimental import pallas as pl
from jax.experimental.pallas import tpu as pltpu
from jax.sharding import PartitionSpec as P

CAP = 10
QUARTERS = 4
FAR = 200.0
APART = 512.0
BF16 = jnp.bfloat16
F32 = jnp.float32
PARAMS = pltpu.CompilerParams(vmem_limit_bytes=48 * 1024 * 1024)
BLOCK = QUARTERS * CAP
GROUP = 8


def mm(a, b):
    return jnp.dot(a, b, preferred_element_type=F32)


def mm_t(a, b):
    return lax.dot_general(a, b, (((1,), (1,)), ((), ())), preferred_element_type=F32)


def place_code(flight):
    rows = np.arange(flight * BLOCK)
    expert, quarter, slot = rows // BLOCK, rows // CAP % QUARTERS, rows % CAP
    code = np.zeros((rows.size, flight + 16), np.float32)
    code[rows, expert] = 1
    code[:, flight] = -slot
    code[rows, flight + 1 + quarter] = APART
    return code


def quarter_code(rows):
    code = np.zeros((16, QUARTERS * rows), np.float32)
    code[0] = 1
    for quarter in range(QUARTERS):
        code[1 + quarter] = np.arange(QUARTERS * rows) // rows != quarter
    return code


def counter(shape, dim):
    return lax.broadcasted_iota(jnp.int32, shape, dim).astype(F32)


def split(number, size):
    quotient = jnp.floor((number + 0.5) * (1.0 / size))
    return quotient, number - size * quotient


def regroup_matrix(back):
    span = GROUP * BLOCK
    row = counter((span, 1), 0)
    if back:
        source, rest = split(row, BLOCK)
        quarter, slot = split(rest, CAP)
        column = quarter * (GROUP * CAP) + source * CAP + slot
    else:
        quarter, rest = split(row, GROUP * CAP)
        source, slot = split(rest, CAP)
        column = source * BLOCK + quarter * CAP + slot
    return jnp.where(counter((span, span), 1) == column, 1.0, 0.0).astype(BF16)


def pack_kernel(flight, ids_ref, token_ref, out_ref):
    top, rows = ids_ref.shape
    places, cols = out_ref.shape
    expert = lax.broadcasted_iota(jnp.int32, (flight, rows), 0)
    named = jnp.zeros((flight, rows), F32)
    for k in range(top):
        named += jnp.where(ids_ref[k : k + 1, :] == expert, 1.0, 0.0)
    earlier = jnp.where(counter((rows, rows), 0) < counter((rows, rows), 1), 1.0, 0.0).astype(BF16)
    slot = jnp.where(named > 0, mm(named.astype(BF16), earlier), FAR)

    line = counter((16, rows), 0)
    other = [jnp.where((line <= QUARTERS) & (line != q + 1), 1.0, 0.0) for q in range(QUARTERS)]
    code = jnp.concatenate([jnp.concatenate([slot, o], axis=0) for o in other], axis=1).astype(BF16)
    place = counter((places, 1), 0) + (pl.program_id(0) * places).astype(F32)
    owner, rest = split(place, BLOCK)
    quarter, place_slot = split(rest, CAP)
    column = counter((places, flight + 16), 1)
    place_code = jnp.where(column == owner, 1.0, 0.0) + jnp.where(column == flight, -place_slot, 0.0)
    place_code += jnp.where(column == flight + 1 + quarter, APART, 0.0)
    gap = mm(place_code.astype(BF16), code)
    selector = jnp.where(gap == 0, 1.0, 0.0).astype(BF16)
    stacked = jnp.concatenate([token_ref[:, q * cols : (q + 1) * cols] for q in range(QUARTERS)], axis=0)
    out_ref[...] = mm(selector, stacked).astype(BF16)


def pack(ids_t, tokens, flight):
    rows, features = tokens.shape
    places = flight * BLOCK
    steps = 4
    whole = lambda a: pl.BlockSpec(a.shape, lambda i: (0, 0))
    return pl.pallas_call(
        functools.partial(pack_kernel, flight),
        out_shape=jax.ShapeDtypeStruct((places, features // QUARTERS), BF16),
        grid=(steps,),
        in_specs=[whole(ids_t), whole(tokens)],
        out_specs=pl.BlockSpec((places // steps, features // QUARTERS), lambda i: (i, 0)),
        compiler_params=pltpu.CompilerParams(vmem_limit_bytes=60 * 1024 * 1024),
        name="pack",
    )(ids_t, tokens)


def first_kernel(order_ref, x_ref, weight_ref, rows_ref, out_ref):
    cols = x_ref.shape[1]
    span, slab = GROUP * BLOCK, GROUP * CAP

    @pl.when(pl.program_id(0) == 0)
    def _():
        regroup = regroup_matrix(False)
        for g in range(x_ref.shape[0] // span):
            sorted_rows = mm(regroup, x_ref[g * span : (g + 1) * span, :]).astype(BF16)
            for q in range(QUARTERS):
                rows_ref[g * slab : (g + 1) * slab, q * cols : (q + 1) * cols] = sorted_rows[q * slab : (q + 1) * slab]

    out_ref[...] = mm_t(rows_ref[...], weight_ref[0, 0]).astype(BF16)


def first_part(order, received, weights):
    places, cols = received.shape
    rows = places // QUARTERS
    features = weights.shape[3]
    units = weights.shape[2]
    whole = lambda shape: pl.BlockSpec(shape, lambda h, order: (0, 0))
    return pl.pallas_call(
        first_kernel,
        out_shape=(jax.ShapeDtypeStruct((rows, features), BF16), jax.ShapeDtypeStruct((rows, 2 * units), BF16)),
        grid_spec=pltpu.PrefetchScalarGridSpec(
            num_scalar_prefetch=1,
            grid=(2,),
            in_specs=[whole((places, cols)),
                      pl.BlockSpec((1, 1, units, features), lambda h, order: (h, order[0], 0, 0))],
            out_specs=(whole((rows, features)), pl.BlockSpec((rows, units), lambda h, order: (0, h))),
        ),
        compiler_params=PARAMS,
        cost_estimate=pl.CostEstimate(flops=4 * rows * units * features, bytes_accessed=4 * units * features, transcendentals=0),
        name="first",
    )(order, received, weights)


def rest_kernel(order_ref, rows_ref, weight_ref, *out_refs):
    units = weight_ref.shape[2]
    for j, out_ref in enumerate(out_refs):
        @pl.when(pl.program_id(0) == j)
        def _():
            for h in range(2):
                out_ref[:, h * units : (h + 1) * units] = mm_t(rows_ref[...], weight_ref[h, 0]).astype(BF16)


def rest_parts(order, rows_in, weights, count):
    rows, features = rows_in.shape
    units = weights.shape[2]
    whole = lambda shape: pl.BlockSpec(shape, lambda i, order: (0, 0))
    return pl.pallas_call(
        rest_kernel,
        out_shape=(jax.ShapeDtypeStruct((rows, 2 * units), BF16),) * count,
        grid_spec=pltpu.PrefetchScalarGridSpec(
            num_scalar_prefetch=1,
            grid=(count,),
            in_specs=[whole((rows, features)),
                      pl.BlockSpec((2, 1, units, features), lambda i, order: (0, order[i], 0, 0))],
            out_specs=(whole((rows, 2 * units)),) * count,
        ),
        compiler_params=PARAMS,
        cost_estimate=pl.CostEstimate(flops=4 * count * rows * units * features, bytes_accessed=4 * count * units * features, transcendentals=0),
        name="rest",
    )(order, rows_in, weights)


def down_kernel(hidden_ref, weight_ref, out_ref):
    cols = out_ref.shape[1]
    span, slab = GROUP * BLOCK, GROUP * CAP
    total = mm(hidden_ref[0], weight_ref[0])
    for k in range(1, hidden_ref.shape[0]):
        total += mm(hidden_ref[k], weight_ref[k])
    total = total.astype(BF16)
    spread = regroup_matrix(True)
    for g in range(out_ref.shape[0] // span):
        block = total[g * slab : (g + 1) * slab, :]
        stacked = jnp.concatenate([block[:, q * cols : (q + 1) * cols] for q in range(QUARTERS)], axis=0)
        out_ref[g * span : (g + 1) * span, :] = mm(spread, stacked).astype(BF16)


def down(hidden, weights):
    parts, rows, units = hidden.shape
    cols = weights.shape[2] // QUARTERS
    vmem = pl.BlockSpec(memory_space=pltpu.VMEM)
    return pl.pallas_call(
        down_kernel,
        out_shape=jax.ShapeDtypeStruct((rows * QUARTERS, cols), BF16),
        in_specs=[vmem, vmem],
        out_specs=vmem,
        compiler_params=pltpu.CompilerParams(vmem_limit_bytes=24 * 1024 * 1024),
        name="down",
    )(hidden, weights)


def mixer_kernel(ids_ref, weight_ref, earlier_ref, expert_ref, slot_ref, quarter_ref, out_ref):
    rows, top = ids_ref.shape
    flight = expert_ref.shape[0]
    expert = lax.broadcasted_iota(jnp.int32, (rows, flight), 1)
    named = jnp.zeros((rows, flight), F32)
    weight = jnp.zeros((rows, flight), F32)
    for k in range(top):
        hit = ids_ref[:, k : k + 1] == expert
        named += jnp.where(hit, 1.0, 0.0)
        weight += jnp.where(hit, weight_ref[:, k : k + 1], 0.0)
    slot = mm(earlier_ref[...], named.astype(BF16))
    slot = jnp.where(named > 0, slot, FAR).astype(BF16)
    gap = mm(slot, expert_ref[...]) + mm(quarter_ref[...], slot_ref[...])
    out_ref[...] = jnp.where(gap == 0, mm(weight.astype(BF16), expert_ref[...]), 0.0).astype(BF16)


def mixer(ids, weight, flight):
    rows = ids.shape[0]
    places = flight * BLOCK
    code = place_code(flight).T
    earlier = jnp.asarray(np.tril(np.ones((rows, rows), np.float32), -1), BF16)
    expert, slot = jnp.asarray(code[:flight], BF16), jnp.asarray(code[flight:], BF16)
    quarter = jnp.asarray(quarter_code(rows).T, BF16)
    whole = lambda a: pl.BlockSpec(a.shape, lambda i: (0, 0))
    return pl.pallas_call(
        mixer_kernel,
        out_shape=jax.ShapeDtypeStruct((QUARTERS * rows, places), BF16),
        grid=(QUARTERS,),
        in_specs=[whole(ids), whole(weight), whole(earlier), whole(expert), whole(slot),
                  pl.BlockSpec((rows, 16), lambda i: (i, 0))],
        out_specs=pl.BlockSpec((rows, places), lambda i: (i, 0)),
        compiler_params=PARAMS,
        name="mixer",
    )(ids, weight, earlier, expert, slot, quarter)


def combine_kernel(mixer_ref, returned_ref, out_ref):
    out_ref[...] = mm(mixer_ref[...], returned_ref[...]).astype(BF16)


def combine(mix, returned):
    places, cols = returned.shape
    rows = mix.shape[0] // QUARTERS
    return pl.pallas_call(
        combine_kernel,
        out_shape=jax.ShapeDtypeStruct((rows, QUARTERS * cols), BF16),
        grid=(QUARTERS,),
        in_specs=[pl.BlockSpec((rows, places), lambda i: (i, 0)), pl.BlockSpec((places, cols), lambda i: (0, 0))],
        out_specs=pl.BlockSpec((rows, cols), lambda i: (0, i)),
        compiler_params=PARAMS,
        name="combine",
    )(mix, returned)


def local(tokens, expert_ids, route_weight, gate_up, down_proj):
    flight = lax.axis_size("ep")
    n_tp = lax.axis_size("tp")
    features = tokens.shape[1]
    cols = features // QUARTERS
    units = gate_up.shape[2] // n_tp
    up_weights = gate_up.reshape(2, n_tp, units, features)
    down_weights = down_proj.reshape(n_tp, units, features)
    me = lax.axis_index("tp")
    order = jnp.stack([me ^ 3, me ^ 1, me ^ 2, me]).astype(jnp.int32)
    near = [(i, i ^ 1) for i in range(n_tp)]
    far = [(i, i ^ 2) for i in range(n_tp)]

    sent = pack(expert_ids.T, tokens, flight)
    received = lax.all_to_all(sent.reshape(flight, BLOCK, cols), "ep", 0, 0, tiled=True).reshape(flight * BLOCK, cols)

    row_block, for_far = first_part(order[:1], received, up_weights)
    got_far = lax.ppermute(for_far, "tp", near)
    for_near, keep_far, keep = rest_parts(order[1:], row_block, up_weights, 3)
    pair_far = (got_far.astype(F32) + keep_far.astype(F32)).astype(BF16)
    for_near, pair_far = lax.optimization_barrier((for_near, pair_far))
    got = lax.ppermute(pair_far, "tp", far)
    got_near = lax.ppermute(for_near, "tp", near)
    summed = got.astype(F32) + got_near.astype(F32) + keep.astype(F32)
    hidden = (jax.nn.silu(summed[:, :units]) * summed[:, units:]).astype(BF16)
    hidden = lax.all_gather(hidden, "tp", axis=0, tiled=False)

    result = down(hidden, down_weights)
    returned = lax.all_to_all(result.reshape(flight, BLOCK, cols), "ep", 0, 0, tiled=True).reshape(flight * BLOCK, cols)
    mix = mixer(expert_ids, route_weight, flight)
    return combine(mix, returned)


def solution(mesh):
    return jax.shard_map(
        local,
        mesh=mesh,
        in_specs=(
            P(("dp", "ep"), "tp"),
            P(("dp", "ep"), None),
            P(("dp", "ep"), None),
            P("ep", None, None, "tp"),
            P("ep", None, "tp"),
        ),
        out_specs=P(("dp", "ep"), "tp"),
        check_vma=False,
    )
```

```python
import functools

import jax
import jax.numpy as jnp
from jax import lax
from jax.experimental import pallas as pl
from jax.experimental.pallas import tpu as pltpu
from jax.sharding import PartitionSpec as P

CAP = 10
QUARTERS = 4
FAR = 200.0
APART = 512.0
BF16 = jnp.bfloat16
F32 = jnp.float32
PARAMS = pltpu.CompilerParams(vmem_limit_bytes=48 * 1024 * 1024)
BLOCK = QUARTERS * CAP
GROUP = 8
HALVES = 2


def mm(a, b):
    return jnp.dot(a, b, preferred_element_type=F32)


def mm_t(a, b):
    return lax.dot_general(a, b, (((1,), (1,)), ((), ())), preferred_element_type=F32)


def counter(shape, dim):
    return lax.broadcasted_iota(jnp.int32, shape, dim).astype(F32)


def split(number, size):
    quotient = jnp.floor((number + 0.5) * (1.0 / size))
    return quotient, number - size * quotient


def regroup_matrix(back):
    span = GROUP * BLOCK
    row = counter((span, 1), 0)
    if back:
        source, rest = split(row, BLOCK)
        quarter, slot = split(rest, CAP)
        column = quarter * (GROUP * CAP) + source * CAP + slot
    else:
        quarter, rest = split(row, GROUP * CAP)
        source, slot = split(rest, CAP)
        column = source * BLOCK + quarter * CAP + slot
    return jnp.where(counter((span, span), 1) == column, 1.0, 0.0).astype(BF16)


def pack_kernel(flight, which_ref, ids_ref, token_ref, out_ref):
    top, rows = ids_ref.shape
    places, cols = out_ref.shape
    expert = lax.broadcasted_iota(jnp.int32, (flight, rows), 0)
    named = jnp.zeros((flight, rows), F32)
    for k in range(top):
        named += jnp.where(ids_ref[k : k + 1, :] == expert, 1.0, 0.0)
    earlier = jnp.where(counter((rows, rows), 0) < counter((rows, rows), 1), 1.0, 0.0).astype(BF16)
    slot = jnp.where(named > 0, mm(named.astype(BF16), earlier), FAR)

    line = counter((16, rows), 0)
    other = [jnp.where((line <= QUARTERS) & (line != q + 1), 1.0, 0.0) for q in range(QUARTERS)]
    code = jnp.concatenate([jnp.concatenate([slot, o], axis=0) for o in other], axis=1).astype(BF16)
    place = counter((places, 1), 0) + (pl.program_id(0) * places).astype(F32)
    pair, rest = split(place, BLOCK)
    owner = HALVES * pair + which_ref[0].astype(F32)
    quarter, place_slot = split(rest, CAP)
    column = counter((places, flight + 16), 1)
    place_code = jnp.where(column == owner, 1.0, 0.0) + jnp.where(column == flight, -place_slot, 0.0)
    place_code += jnp.where(column == flight + 1 + quarter, APART, 0.0)
    gap = mm(place_code.astype(BF16), code)
    selector = jnp.where(gap == 0, 1.0, 0.0).astype(BF16)
    stacked = jnp.concatenate([token_ref[:, q * cols : (q + 1) * cols] for q in range(QUARTERS)], axis=0)
    out_ref[...] = mm(selector, stacked).astype(BF16)


def pack(which, ids_t, tokens, flight):
    rows, features = tokens.shape
    places = flight // HALVES * BLOCK
    steps = 2
    whole = lambda a: pl.BlockSpec(a.shape, lambda i, which: (0, 0))
    return pl.pallas_call(
        functools.partial(pack_kernel, flight),
        out_shape=jax.ShapeDtypeStruct((places, features // QUARTERS), BF16),
        grid_spec=pltpu.PrefetchScalarGridSpec(
            num_scalar_prefetch=1,
            grid=(steps,),
            in_specs=[whole(ids_t), whole(tokens)],
            out_specs=pl.BlockSpec((places // steps, features // QUARTERS), lambda i, which: (i, 0)),
        ),
        compiler_params=pltpu.CompilerParams(vmem_limit_bytes=60 * 1024 * 1024),
        name="pack",
    )(which, ids_t, tokens)


def first_kernel(order_ref, x_ref, weight_ref, rows_ref, out_ref):
    cols = x_ref.shape[1]
    span, slab = GROUP * BLOCK, GROUP * CAP

    @pl.when(pl.program_id(0) == 0)
    def _():
        regroup = regroup_matrix(False)
        for g in range(x_ref.shape[0] // span):
            sorted_rows = mm(regroup, x_ref[g * span : (g + 1) * span, :]).astype(BF16)
            for q in range(QUARTERS):
                rows_ref[g * slab : (g + 1) * slab, q * cols : (q + 1) * cols] = sorted_rows[q * slab : (q + 1) * slab]

    out_ref[...] = mm_t(rows_ref[...], weight_ref[0, 0]).astype(BF16)


def first_part(order, received, weights):
    places, cols = received.shape
    rows = places // QUARTERS
    features = weights.shape[3]
    units = weights.shape[2]
    whole = lambda shape: pl.BlockSpec(shape, lambda h, order: (0, 0))
    return pl.pallas_call(
        first_kernel,
        out_shape=(jax.ShapeDtypeStruct((rows, features), BF16), jax.ShapeDtypeStruct((rows, 2 * units), BF16)),
        grid_spec=pltpu.PrefetchScalarGridSpec(
            num_scalar_prefetch=1,
            grid=(2,),
            in_specs=[whole((places, cols)),
                      pl.BlockSpec((1, 1, units, features), lambda h, order: (h, order[0], 0, 0))],
            out_specs=(whole((rows, features)), pl.BlockSpec((rows, units), lambda h, order: (0, h))),
        ),
        compiler_params=PARAMS,
        cost_estimate=pl.CostEstimate(flops=4 * rows * units * features, bytes_accessed=4 * units * features, transcendentals=0),
        name="first",
    )(order, received, weights)


def rest_kernel(order_ref, rows_ref, weight_ref, *out_refs):
    units = weight_ref.shape[2]
    for j, out_ref in enumerate(out_refs):
        @pl.when(pl.program_id(0) == j)
        def _():
            for h in range(2):
                out_ref[:, h * units : (h + 1) * units] = mm_t(rows_ref[...], weight_ref[h, 0]).astype(BF16)


def rest_parts(order, rows_in, weights, count):
    rows, features = rows_in.shape
    units = weights.shape[2]
    whole = lambda shape: pl.BlockSpec(shape, lambda i, order: (0, 0))
    return pl.pallas_call(
        rest_kernel,
        out_shape=(jax.ShapeDtypeStruct((rows, 2 * units), BF16),) * count,
        grid_spec=pltpu.PrefetchScalarGridSpec(
            num_scalar_prefetch=1,
            grid=(count,),
            in_specs=[whole((rows, features)),
                      pl.BlockSpec((2, 1, units, features), lambda i, order: (0, order[i], 0, 0))],
            out_specs=(whole((rows, 2 * units)),) * count,
        ),
        compiler_params=PARAMS,
        cost_estimate=pl.CostEstimate(flops=4 * count * rows * units * features, bytes_accessed=4 * count * units * features, transcendentals=0),
        name="rest",
    )(order, rows_in, weights)


def down_kernel(order_ref, *refs):
    *hidden_refs, weight_ref, out_ref = refs
    cols = out_ref.shape[1]
    span, slab = GROUP * BLOCK, GROUP * CAP
    total = mm(hidden_refs[0][...], weight_ref[order_ref[0]])
    for k in range(1, len(hidden_refs)):
        total += mm(hidden_refs[k][...], weight_ref[order_ref[k]])
    total = total.astype(BF16)
    spread = regroup_matrix(True)
    for g in range(out_ref.shape[0] // span):
        block = total[g * slab : (g + 1) * slab, :]
        stacked = jnp.concatenate([block[:, q * cols : (q + 1) * cols] for q in range(QUARTERS)], axis=0)
        out_ref[g * span : (g + 1) * span, :] = mm(spread, stacked).astype(BF16)


def down(order, hidden, weights):
    rows = hidden[0].shape[0]
    cols = weights.shape[2] // QUARTERS
    vmem = pl.BlockSpec(memory_space=pltpu.VMEM)
    return pl.pallas_call(
        down_kernel,
        out_shape=jax.ShapeDtypeStruct((rows * QUARTERS, cols), BF16),
        in_specs=[pl.BlockSpec(memory_space=pltpu.SMEM)] + [vmem] * (len(hidden) + 1),
        out_specs=vmem,
        compiler_params=pltpu.CompilerParams(vmem_limit_bytes=24 * 1024 * 1024),
        cost_estimate=pl.CostEstimate(flops=2 * rows * weights.size, bytes_accessed=2 * weights.size, transcendentals=0),
        name="down",
    )(order, *hidden, weights)


def mixer_kernel(flight, half_ref, ids_ref, weight_ref, out_ref):
    rows, top = ids_ref.shape
    places = out_ref.shape[1]
    expert = lax.broadcasted_iota(jnp.int32, (rows, flight), 1)
    named = jnp.zeros((rows, flight), F32)
    weight = jnp.zeros((rows, flight), F32)
    for k in range(top):
        hit = ids_ref[:, k : k + 1] == expert
        named += jnp.where(hit, 1.0, 0.0)
        weight += jnp.where(hit, weight_ref[:, k : k + 1], 0.0)
    earlier = jnp.where(counter((rows, rows), 1) < counter((rows, rows), 0), 1.0, 0.0).astype(BF16)
    slot = mm(earlier, named.astype(BF16))
    slot = jnp.where(named > 0, slot, FAR).astype(BF16)

    part, rest = split(counter((1, places), 1), places // HALVES)
    pair, rest = split(rest, BLOCK)
    quarter, place_slot = split(rest, CAP)
    half = half_ref[0].astype(F32)
    owner = HALVES * pair + jnp.where(part == 0, half, HALVES - 1 - half)
    owned = jnp.where(counter((flight, places), 0) == owner, 1.0, 0.0).astype(BF16)
    here = quarter == pl.program_id(0).astype(F32)
    gap = mm(slot, owned) - jnp.where(here, place_slot, -1.0)
    out_ref[...] = jnp.where(gap == 0, mm(weight.astype(BF16), owned), 0.0).astype(BF16)


def mixer(half, ids, weight, flight):
    rows = ids.shape[0]
    places = flight * BLOCK
    whole = lambda a: pl.BlockSpec(a.shape, lambda i, half: (0, 0))
    return pl.pallas_call(
        functools.partial(mixer_kernel, flight),
        out_shape=jax.ShapeDtypeStruct((QUARTERS * rows, places), BF16),
        grid_spec=pltpu.PrefetchScalarGridSpec(
            num_scalar_prefetch=1,
            grid=(QUARTERS,),
            in_specs=[whole(ids), whole(weight)],
            out_specs=pl.BlockSpec((rows, places), lambda i, half: (i, 0)),
        ),
        compiler_params=pltpu.CompilerParams(vmem_limit_bytes=24 * 1024 * 1024),
        name="mixer",
    )(half, ids, weight)


def combine_kernel(mixer_ref, same_ref, other_ref, out_ref):
    places = same_ref.shape[0]
    total = mm(mixer_ref[:, :places], same_ref[...]) + mm(mixer_ref[:, places:], other_ref[...])
    out_ref[...] = total.astype(BF16)


def combine(mix, same, other):
    places, cols = same.shape
    rows = mix.shape[0] // QUARTERS
    returned = pl.BlockSpec((places, cols), lambda i: (0, 0))
    return pl.pallas_call(
        combine_kernel,
        out_shape=jax.ShapeDtypeStruct((rows, QUARTERS * cols), BF16),
        grid=(QUARTERS,),
        in_specs=[pl.BlockSpec((rows, mix.shape[1]), lambda i: (i, 0)), returned, returned],
        out_specs=pl.BlockSpec((rows, cols), lambda i: (0, i)),
        compiler_params=pltpu.CompilerParams(vmem_limit_bytes=24 * 1024 * 1024),
        name="combine",
    )(mix, same, other)


def tie(*values):
    return lax.optimization_barrier(values)


def local(tokens, expert_ids, route_weight, gate_up, down_proj):
    flight = lax.axis_size("ep")
    n_tp = lax.axis_size("tp")
    features = tokens.shape[1]
    cols = features // QUARTERS
    units = gate_up.shape[2] // n_tp
    up_weights = gate_up.reshape(2, n_tp, units, features)
    down_weights = down_proj.reshape(n_tp, units, features)
    me = lax.axis_index("tp")
    half = lax.axis_index("ep") % HALVES
    order = jnp.stack([me ^ 3, me ^ 1, me ^ 2, me]).astype(jnp.int32)
    same_half = jnp.stack([half]).astype(jnp.int32)
    other_half = jnp.stack([1 - half]).astype(jnp.int32)
    near = [(i, i ^ 1) for i in range(n_tp)]
    far = [(i, i ^ 2) for i in range(n_tp)]
    cross = [(i, i ^ 3) for i in range(n_tp)]
    lines = [list(range(h, flight, HALVES)) for h in range(HALVES)]
    swap = [(i, i ^ 1) for i in range(flight)]

    def exchange(rows):
        blocks = rows.reshape(flight // HALVES, BLOCK, cols)
        return lax.all_to_all(blocks, "ep", 0, 0, axis_index_groups=lines, tiled=True).reshape(rows.shape)

    def swapped(rows):
        return lax.ppermute(rows, "ep", swap)

    def pair_sum(got_far, keep_far):
        return (got_far.astype(F32) + keep_far.astype(F32)).astype(BF16)

    def activated(got, got_near, keep):
        summed = got.astype(F32) + got_near.astype(F32) + keep.astype(F32)
        return (jax.nn.silu(summed[:, :units]) * summed[:, units:]).astype(BF16)

    def gathered(hidden):
        return [lax.ppermute(hidden, "tp", pairs) for pairs in (cross, near, far)] + [hidden]

    for_other = pack(other_half, expert_ids.T, tokens, flight)
    crossed = swapped(for_other)
    for_same = pack(same_half, expert_ids.T, tokens, flight)
    received = exchange(for_same)
    received, crossed = tie(received, crossed)
    received_2 = exchange(crossed)

    rows, for_far = first_part(order[:1], received, up_weights)
    got_far = lax.ppermute(for_far, "tp", near)
    for_near, keep_far, keep = rest_parts(order[1:], rows, up_weights, 3)
    pair_far, for_near = tie(pair_sum(got_far, keep_far), for_near)
    got = lax.ppermute(pair_far, "tp", far)
    got_near = lax.ppermute(for_near, "tp", near)

    received_2, pair_far = tie(received_2, pair_far)
    rows_2, for_far_2 = first_part(order[:1], received_2, up_weights)
    got_far_2 = lax.ppermute(for_far_2, "tp", near)
    for_near_2, keep_far_2, keep_2 = rest_parts(order[1:], rows_2, up_weights, 3)

    got, got_near, keep, keep_2 = tie(got, got_near, keep, keep_2)
    parts = gathered(activated(got, got_near, keep))
    pair_far_2, for_near_2 = tie(pair_sum(got_far_2, keep_far_2), for_near_2)
    got_2 = lax.ppermute(pair_far_2, "tp", far)
    got_near_2 = lax.ppermute(for_near_2, "tp", near)

    parts, pair_far_2 = tie(parts, pair_far_2)
    result = down(order, parts, down_weights)
    returned = exchange(result)
    got_2, got_near_2, result = tie(got_2, got_near_2, result)
    parts_2 = gathered(activated(got_2, got_near_2, keep_2))
    result_2 = down(order, parts_2, down_weights)
    result_2, returned = tie(result_2, returned)
    returned_2 = swapped(exchange(result_2))
    result_2, ids, weight = tie(result_2, expert_ids, route_weight)
    mix = mixer(same_half, ids, weight, flight)
    return combine(mix, returned, returned_2)


def solution(mesh):
    return jax.shard_map(
        local,
        mesh=mesh,
        in_specs=(
            P(("dp", "ep"), "tp"),
            P(("dp", "ep"), None),
            P(("dp", "ep"), None),
            P("ep", None, None, "tp"),
            P("ep", None, "tp"),
        ),
        out_specs=P(("dp", "ep"), "tp"),
        check_vma=False,
    )
```

```python
import functools

import jax
import jax.numpy as jnp
import numpy as np
from jax import lax
from jax.experimental import pallas as pl
from jax.experimental.pallas import tpu as pltpu
from jax.sharding import PartitionSpec as P

CAP = 10
QUARTERS = 4
FAR = 200.0
APART = 512.0
BF16 = jnp.bfloat16
F32 = jnp.float32
PARAMS = pltpu.CompilerParams(vmem_limit_bytes=48 * 1024 * 1024)
BLOCK = QUARTERS * CAP
GROUP = 8
PIECE = 128


def mm(a, b):
    return jnp.dot(a, b, preferred_element_type=F32)


def mm_t(a, b):
    return lax.dot_general(a, b, (((1,), (1,)), ((), ())), preferred_element_type=F32)


def place_code(flight):
    rows = np.arange(flight * BLOCK)
    expert, quarter, slot = rows // BLOCK, rows // CAP % QUARTERS, rows % CAP
    code = np.zeros((rows.size, flight + 16), np.float32)
    code[rows, expert] = 1
    code[:, flight] = -slot
    code[rows, flight + 1 + quarter] = APART
    return code


def quarter_code(rows):
    code = np.zeros((16, QUARTERS * rows), np.float32)
    code[0] = 1
    for quarter in range(QUARTERS):
        code[1 + quarter] = np.arange(QUARTERS * rows) // rows != quarter
    return code


def counter(shape, dim):
    return lax.broadcasted_iota(jnp.int32, shape, dim).astype(F32)


def split(number, size):
    quotient = jnp.floor((number + 0.5) * (1.0 / size))
    return quotient, number - size * quotient


def regroup_matrix(back):
    span = GROUP * BLOCK
    row = counter((span, 1), 0)
    if back:
        source, rest = split(row, BLOCK)
        quarter, slot = split(rest, CAP)
        column = quarter * (GROUP * CAP) + source * CAP + slot
    else:
        quarter, rest = split(row, GROUP * CAP)
        source, slot = split(rest, CAP)
        column = source * BLOCK + quarter * CAP + slot
    return jnp.where(counter((span, span), 1) == column, 1.0, 0.0).astype(BF16)


def pack_kernel(flight, ids_ref, token_ref, out_ref):
    top, rows = ids_ref.shape
    places, cols = out_ref.shape
    expert = lax.broadcasted_iota(jnp.int32, (flight, rows), 0)
    named = jnp.zeros((flight, rows), F32)
    for k in range(top):
        named += jnp.where(ids_ref[k : k + 1, :] == expert, 1.0, 0.0)
    earlier = jnp.where(counter((rows, rows), 0) < counter((rows, rows), 1), 1.0, 0.0).astype(BF16)
    slot = jnp.where(named > 0, mm(named.astype(BF16), earlier), FAR)

    line = counter((16, rows), 0)
    other = [jnp.where((line <= QUARTERS) & (line != q + 1), 1.0, 0.0) for q in range(QUARTERS)]
    code = jnp.concatenate([jnp.concatenate([slot, o], axis=0) for o in other], axis=1).astype(BF16)
    place = counter((places, 1), 0) + (pl.program_id(0) * places).astype(F32)
    owner, rest = split(place, BLOCK)
    quarter, place_slot = split(rest, CAP)
    column = counter((places, flight + 16), 1)
    place_code = jnp.where(column == owner, 1.0, 0.0) + jnp.where(column == flight, -place_slot, 0.0)
    place_code += jnp.where(column == flight + 1 + quarter, APART, 0.0)
    gap = mm(place_code.astype(BF16), code)
    selector = jnp.where(gap == 0, 1.0, 0.0).astype(BF16)
    stacked = jnp.concatenate([token_ref[:, q * cols : (q + 1) * cols] for q in range(QUARTERS)], axis=0)
    out_ref[...] = mm(selector, stacked).astype(BF16)


def pack(ids_t, tokens, flight):
    rows, features = tokens.shape
    places = flight * BLOCK
    steps = 2
    whole = lambda a: pl.BlockSpec(a.shape, lambda i: (0, 0))
    return pl.pallas_call(
        functools.partial(pack_kernel, flight),
        out_shape=jax.ShapeDtypeStruct((places, features // QUARTERS), BF16),
        grid=(steps,),
        in_specs=[whole(ids_t), whole(tokens)],
        out_specs=pl.BlockSpec((places // steps, features // QUARTERS), lambda i: (i, 0)),
        compiler_params=pltpu.CompilerParams(vmem_limit_bytes=60 * 1024 * 1024),
        name="pack",
    )(ids_t, tokens)


def first_kernel(me_ref, x_ref, weight_ref, rows_ref, out_ref):
    cols = x_ref.shape[1]
    span, slab = GROUP * BLOCK, GROUP * CAP
    regroup = regroup_matrix(False)
    for g in range(x_ref.shape[0] // span):
        sorted_rows = mm(regroup, x_ref[g * span : (g + 1) * span, :]).astype(BF16)
        for q in range(QUARTERS):
            rows_ref[g * slab : (g + 1) * slab, q * cols : (q + 1) * cols] = sorted_rows[q * slab : (q + 1) * slab]
    out_ref[...] = mm_t(rows_ref[...], weight_ref[...].reshape(2 * PIECE, -1)).astype(BF16)


def piece_of(weights, quarter, mask, piece):
    return (quarter ^ mask) * (weights.shape[1] // QUARTERS) + piece


def first_part(me, mask, received, weights):
    places, cols = received.shape
    rows = places // QUARTERS
    features = weights.shape[3]
    whole = lambda shape: pl.BlockSpec(shape, lambda i, me: (0, 0))
    return pl.pallas_call(
        first_kernel,
        out_shape=(jax.ShapeDtypeStruct((rows, features), BF16), jax.ShapeDtypeStruct((rows, 2 * PIECE), BF16)),
        grid_spec=pltpu.PrefetchScalarGridSpec(
            num_scalar_prefetch=1,
            grid=(1,),
            in_specs=[whole((places, cols)),
                      pl.BlockSpec((2, 1, PIECE, features), lambda i, me: (0, piece_of(weights, me[0], mask, 0), 0, 0))],
            out_specs=(whole((rows, features)), whole((rows, 2 * PIECE))),
        ),
        compiler_params=PARAMS,
        cost_estimate=pl.CostEstimate(flops=4 * rows * PIECE * features, bytes_accessed=4 * PIECE * features, transcendentals=0),
        name="first",
    )(me, received, weights)


def parts_kernel(pieces, me_ref, rows_ref, weight_ref, *out_refs):
    steps = [(out_ref, p) for out_ref, count in zip(out_refs, pieces) for p in range(count)]
    for i, (out_ref, p) in enumerate(steps):
        @pl.when(pl.program_id(0) == i)
        def _():
            product = mm_t(rows_ref[...], weight_ref[...].reshape(2 * PIECE, -1))
            out_ref[:, p * 2 * PIECE : (p + 1) * 2 * PIECE] = product.astype(BF16)


def parts(me, mask, rows_in, weights, *pieces, start=0):
    rows, features = rows_in.shape
    steps = sum(pieces)
    whole = lambda shape: pl.BlockSpec(shape, lambda i, me: (0, 0))
    shapes = [(rows, 2 * PIECE * count) for count in pieces]
    return pl.pallas_call(
        functools.partial(parts_kernel, pieces),
        out_shape=tuple(jax.ShapeDtypeStruct(shape, BF16) for shape in shapes),
        grid_spec=pltpu.PrefetchScalarGridSpec(
            num_scalar_prefetch=1,
            grid=(steps,),
            in_specs=[whole((rows, features)),
                      pl.BlockSpec((2, 1, PIECE, features), lambda i, me: (0, piece_of(weights, me[0], mask, start + i), 0, 0))],
            out_specs=tuple(whole(shape) for shape in shapes),
        ),
        compiler_params=PARAMS,
        cost_estimate=pl.CostEstimate(flops=4 * steps * rows * PIECE * features, bytes_accessed=4 * steps * PIECE * features, transcendentals=0),
        name="parts",
    )(me, rows_in, weights)


def down_kernel(hidden_ref, weight_ref, out_ref):
    cols = out_ref.shape[1]
    span, slab = GROUP * BLOCK, GROUP * CAP
    total = mm(hidden_ref[0], weight_ref[0])
    for k in range(1, hidden_ref.shape[0]):
        total += mm(hidden_ref[k], weight_ref[k])
    total = total.astype(BF16)
    spread = regroup_matrix(True)
    for g in range(out_ref.shape[0] // span):
        block = total[g * slab : (g + 1) * slab, :]
        stacked = jnp.concatenate([block[:, q * cols : (q + 1) * cols] for q in range(QUARTERS)], axis=0)
        out_ref[g * span : (g + 1) * span, :] = mm(spread, stacked).astype(BF16)


def down(hidden, weights):
    parts, rows, units = hidden.shape
    cols = weights.shape[2] // QUARTERS
    vmem = pl.BlockSpec(memory_space=pltpu.VMEM)
    return pl.pallas_call(
        down_kernel,
        out_shape=jax.ShapeDtypeStruct((rows * QUARTERS, cols), BF16),
        in_specs=[vmem, vmem],
        out_specs=vmem,
        compiler_params=pltpu.CompilerParams(vmem_limit_bytes=24 * 1024 * 1024),
        name="down",
    )(hidden, weights)


def mixer_kernel(ids_ref, weight_ref, earlier_ref, expert_ref, slot_ref, quarter_ref, out_ref):
    rows, top = ids_ref.shape
    flight = expert_ref.shape[0]
    expert = lax.broadcasted_iota(jnp.int32, (rows, flight), 1)
    named = jnp.zeros((rows, flight), F32)
    weight = jnp.zeros((rows, flight), F32)
    for k in range(top):
        hit = ids_ref[:, k : k + 1] == expert
        named += jnp.where(hit, 1.0, 0.0)
        weight += jnp.where(hit, weight_ref[:, k : k + 1], 0.0)
    slot = mm(earlier_ref[...], named.astype(BF16))
    slot = jnp.where(named > 0, slot, FAR).astype(BF16)
    gap = mm(slot, expert_ref[...]) + mm(quarter_ref[...], slot_ref[...])
    out_ref[...] = jnp.where(gap == 0, mm(weight.astype(BF16), expert_ref[...]), 0.0).astype(BF16)


def mixer(ids, weight, flight):
    rows = ids.shape[0]
    places = flight * BLOCK
    code = place_code(flight).T
    earlier = jnp.asarray(np.tril(np.ones((rows, rows), np.float32), -1), BF16)
    expert, slot = jnp.asarray(code[:flight], BF16), jnp.asarray(code[flight:], BF16)
    quarter = jnp.asarray(quarter_code(rows).T, BF16)
    whole = lambda a: pl.BlockSpec(a.shape, lambda i: (0, 0))
    return pl.pallas_call(
        mixer_kernel,
        out_shape=jax.ShapeDtypeStruct((QUARTERS * rows, places), BF16),
        grid=(QUARTERS,),
        in_specs=[whole(ids), whole(weight), whole(earlier), whole(expert), whole(slot),
                  pl.BlockSpec((rows, 16), lambda i: (i, 0))],
        out_specs=pl.BlockSpec((rows, places), lambda i: (i, 0)),
        compiler_params=PARAMS,
        name="mixer",
    )(ids, weight, earlier, expert, slot, quarter)


def combine_kernel(mixer_ref, returned_ref, out_ref):
    out_ref[...] = mm(mixer_ref[...], returned_ref[...]).astype(BF16)


def combine(mix, returned):
    places, cols = returned.shape
    rows = mix.shape[0] // QUARTERS
    return pl.pallas_call(
        combine_kernel,
        out_shape=jax.ShapeDtypeStruct((rows, QUARTERS * cols), BF16),
        grid=(QUARTERS,),
        in_specs=[pl.BlockSpec((rows, places), lambda i: (i, 0)), pl.BlockSpec((places, cols), lambda i: (0, 0))],
        out_specs=pl.BlockSpec((rows, cols), lambda i: (0, i)),
        compiler_params=PARAMS,
        name="combine",
    )(mix, returned)


def tie(*values):
    return lax.optimization_barrier(values)


def local(tokens, expert_ids, route_weight, gate_up, down_proj):
    flight = lax.axis_size("ep")
    n_tp = lax.axis_size("tp")
    features = tokens.shape[1]
    cols = features // QUARTERS
    units = gate_up.shape[2] // n_tp
    pieces = units // PIECE
    up_weights = gate_up.reshape(2, n_tp * pieces, PIECE, features)
    down_weights = down_proj.reshape(n_tp, units, features)
    me = lax.axis_index("tp").astype(jnp.int32).reshape(1)
    near = [(i, i ^ 1) for i in range(n_tp)]
    far = [(i, i ^ 2) for i in range(n_tp)]

    def pair_sum(got, keep):
        return (got.astype(F32) + keep.astype(F32)).astype(BF16)

    sent = pack(expert_ids.T, tokens, flight)
    received = lax.all_to_all(sent.reshape(flight, BLOCK, cols), "ep", 0, 0, tiled=True).reshape(flight * BLOCK, cols)

    rows, far_1 = first_part(me, 3, received, up_weights)
    got_1 = lax.ppermute(far_1, "tp", near)
    (far_2,) = parts(me, 3, rows, up_weights, pieces - 1, start=1)
    got_2 = lax.ppermute(far_2, "tp", near)
    rows, far_2 = tie(rows, far_2)
    keep_1, keep_2 = parts(me, 2, rows, up_weights, 1, pieces - 1)
    pair_1 = pair_sum(got_1, keep_1)
    rows, pair_1 = tie(rows, pair_1)
    got_1 = lax.ppermute(pair_1, "tp", far)
    (for_near,) = parts(me, 1, rows, up_weights, pieces)
    got_near = lax.ppermute(for_near, "tp", near)
    for_near, got_2 = tie(for_near, got_2)
    pair_2 = pair_sum(got_2, keep_2)
    rows, pair_2, got_1 = tie(rows, pair_2, got_1)
    got_2 = lax.ppermute(pair_2, "tp", far)
    (keep,) = parts(me, 0, rows, up_weights, pieces)
    got = [got_1] + [got_2[:, p * 2 * PIECE : (p + 1) * 2 * PIECE] for p in range(pieces - 1)]
    hidden = []
    for p in range(pieces):
        columns = slice(p * 2 * PIECE, (p + 1) * 2 * PIECE)
        summed = got[p].astype(F32) + got_near[:, columns].astype(F32) + keep[:, columns].astype(F32)
        hidden.append((jax.nn.silu(summed[:, :PIECE]) * summed[:, PIECE:]).astype(BF16))
    hidden = lax.all_gather(jnp.concatenate(hidden, axis=1), "tp", axis=0, tiled=False)

    result = down(hidden, down_weights)
    returned = lax.all_to_all(result.reshape(flight, BLOCK, cols), "ep", 0, 0, tiled=True).reshape(flight * BLOCK, cols)
    mix = mixer(expert_ids, route_weight, flight)
    return combine(mix, returned)


def solution(mesh):
    return jax.shard_map(
        local,
        mesh=mesh,
        in_specs=(
            P(("dp", "ep"), "tp"),
            P(("dp", "ep"), None),
            P(("dp", "ep"), None),
            P("ep", None, None, "tp"),
            P("ep", None, "tp"),
        ),
        out_specs=P(("dp", "ep"), "tp"),
        check_vma=False,
    )
```

```python
import functools

import jax
import jax.numpy as jnp
import numpy as np
from jax import lax
from jax.experimental import pallas as pl
from jax.experimental.pallas import tpu as pltpu
from jax.sharding import PartitionSpec as P

CAP = 10
QUARTERS = 4
FAR = 200.0
APART = 512.0
BF16 = jnp.bfloat16
F32 = jnp.float32
PARAMS = pltpu.CompilerParams(vmem_limit_bytes=48 * 1024 * 1024)
BLOCK = QUARTERS * CAP
GROUP = 8
PIECE = 128


def mm(a, b):
    return jnp.dot(a, b, preferred_element_type=F32)


def mm_t(a, b):
    return lax.dot_general(a, b, (((1,), (1,)), ((), ())), preferred_element_type=F32)


def place_code(flight):
    rows = np.arange(flight * BLOCK)
    expert, quarter, slot = rows // BLOCK, rows // CAP % QUARTERS, rows % CAP
    code = np.zeros((rows.size, flight + 16), np.float32)
    code[rows, expert] = 1
    code[:, flight] = -slot
    code[rows, flight + 1 + quarter] = APART
    return code


def quarter_code(rows):
    code = np.zeros((16, QUARTERS * rows), np.float32)
    code[0] = 1
    for quarter in range(QUARTERS):
        code[1 + quarter] = np.arange(QUARTERS * rows) // rows != quarter
    return code


def counter(shape, dim):
    return lax.broadcasted_iota(jnp.int32, shape, dim).astype(F32)


def split(number, size):
    quotient = jnp.floor((number + 0.5) * (1.0 / size))
    return quotient, number - size * quotient


def regroup_matrix(back):
    span = GROUP * BLOCK
    row = counter((span, 1), 0)
    if back:
        source, rest = split(row, BLOCK)
        quarter, slot = split(rest, CAP)
        column = quarter * (GROUP * CAP) + source * CAP + slot
    else:
        quarter, rest = split(row, GROUP * CAP)
        source, slot = split(rest, CAP)
        column = source * BLOCK + quarter * CAP + slot
    return jnp.where(counter((span, span), 1) == column, 1.0, 0.0).astype(BF16)


def pack_kernel(flight, ids_ref, token_ref, out_ref):
    top, rows = ids_ref.shape
    places, cols = out_ref.shape
    expert = lax.broadcasted_iota(jnp.int32, (flight, rows), 0)
    named = jnp.zeros((flight, rows), F32)
    for k in range(top):
        named += jnp.where(ids_ref[k : k + 1, :] == expert, 1.0, 0.0)
    earlier = jnp.where(counter((rows, rows), 0) < counter((rows, rows), 1), 1.0, 0.0).astype(BF16)
    slot = jnp.where(named > 0, mm(named.astype(BF16), earlier), FAR)

    line = counter((16, rows), 0)
    other = [jnp.where((line <= QUARTERS) & (line != q + 1), 1.0, 0.0) for q in range(QUARTERS)]
    code = jnp.concatenate([jnp.concatenate([slot, o], axis=0) for o in other], axis=1).astype(BF16)
    place = counter((places, 1), 0) + (pl.program_id(0) * places).astype(F32)
    owner, rest = split(place, BLOCK)
    quarter, place_slot = split(rest, CAP)
    column = counter((places, flight + 16), 1)
    place_code = jnp.where(column == owner, 1.0, 0.0) + jnp.where(column == flight, -place_slot, 0.0)
    place_code += jnp.where(column == flight + 1 + quarter, APART, 0.0)
    gap = mm(place_code.astype(BF16), code)
    selector = jnp.where(gap == 0, 1.0, 0.0).astype(BF16)
    stacked = jnp.concatenate([token_ref[:, q * cols : (q + 1) * cols] for q in range(QUARTERS)], axis=0)
    out_ref[...] = mm(selector, stacked).astype(BF16)


def pack(ids_t, tokens, flight):
    rows, features = tokens.shape
    places = flight * BLOCK
    steps = 2
    whole = lambda a: pl.BlockSpec(a.shape, lambda i: (0, 0))
    return pl.pallas_call(
        functools.partial(pack_kernel, flight),
        out_shape=jax.ShapeDtypeStruct((places, features // QUARTERS), BF16),
        grid=(steps,),
        in_specs=[whole(ids_t), whole(tokens)],
        out_specs=pl.BlockSpec((places // steps, features // QUARTERS), lambda i: (i, 0)),
        compiler_params=pltpu.CompilerParams(vmem_limit_bytes=60 * 1024 * 1024),
        name="pack",
    )(ids_t, tokens)


def first_kernel(me_ref, x_ref, weight_ref, rows_ref, first_ref, rest_ref):
    cols = x_ref.shape[1]
    span, slab = GROUP * BLOCK, GROUP * CAP
    step = pl.program_id(0)

    @pl.when(step == 0)
    def _():
        regroup = regroup_matrix(False)
        for g in range(x_ref.shape[0] // span):
            sorted_rows = mm(regroup, x_ref[g * span : (g + 1) * span, :]).astype(BF16)
            for q in range(QUARTERS):
                rows_ref[g * slab : (g + 1) * slab, q * cols : (q + 1) * cols] = sorted_rows[q * slab : (q + 1) * slab]

    product = mm_t(rows_ref[...], weight_ref[...].reshape(2 * PIECE, -1)).astype(BF16)

    @pl.when(step == 0)
    def _():
        first_ref[...] = product

    for p in range(rest_ref.shape[1] // (2 * PIECE)):
        @pl.when(step == p + 1)
        def _():
            rest_ref[:, p * 2 * PIECE : (p + 1) * 2 * PIECE] = product


def piece_of(weights, quarter, mask, piece):
    return (quarter ^ mask) * (weights.shape[1] // QUARTERS) + piece


def first_part(me, mask, received, weights):
    places, cols = received.shape
    rows = places // QUARTERS
    features = weights.shape[3]
    pieces = weights.shape[1] // QUARTERS
    whole = lambda shape: pl.BlockSpec(shape, lambda i, me: (0, 0))
    shapes = [(rows, features), (rows, 2 * PIECE), (rows, 2 * PIECE * (pieces - 1))]
    return pl.pallas_call(
        first_kernel,
        out_shape=tuple(jax.ShapeDtypeStruct(shape, BF16) for shape in shapes),
        grid_spec=pltpu.PrefetchScalarGridSpec(
            num_scalar_prefetch=1,
            grid=(pieces,),
            in_specs=[whole((places, cols)),
                      pl.BlockSpec((2, 1, PIECE, features), lambda i, me: (0, piece_of(weights, me[0], mask, i), 0, 0))],
            out_specs=tuple(whole(shape) for shape in shapes),
        ),
        compiler_params=PARAMS,
        cost_estimate=pl.CostEstimate(flops=4 * rows * pieces * PIECE * features, bytes_accessed=4 * pieces * PIECE * features, transcendentals=0),
        name="first",
    )(me, received, weights)


def parts_kernel(pieces, me_ref, rows_ref, weight_ref, *out_refs):
    steps = [(out_ref, p) for out_ref, count in zip(out_refs, pieces) for p in range(count)]
    for i, (out_ref, p) in enumerate(steps):
        @pl.when(pl.program_id(0) == i)
        def _():
            product = mm_t(rows_ref[...], weight_ref[...].reshape(2 * PIECE, -1))
            out_ref[:, p * 2 * PIECE : (p + 1) * 2 * PIECE] = product.astype(BF16)


def parts(me, mask, rows_in, weights, *pieces, start=0):
    rows, features = rows_in.shape
    steps = sum(pieces)
    whole = lambda shape: pl.BlockSpec(shape, lambda i, me: (0, 0))
    shapes = [(rows, 2 * PIECE * count) for count in pieces]
    return pl.pallas_call(
        functools.partial(parts_kernel, pieces),
        out_shape=tuple(jax.ShapeDtypeStruct(shape, BF16) for shape in shapes),
        grid_spec=pltpu.PrefetchScalarGridSpec(
            num_scalar_prefetch=1,
            grid=(steps,),
            in_specs=[whole((rows, features)),
                      pl.BlockSpec((2, 1, PIECE, features), lambda i, me: (0, piece_of(weights, me[0], mask, start + i), 0, 0))],
            out_specs=tuple(whole(shape) for shape in shapes),
        ),
        compiler_params=PARAMS,
        cost_estimate=pl.CostEstimate(flops=4 * steps * rows * PIECE * features, bytes_accessed=4 * steps * PIECE * features, transcendentals=0),
        name="parts",
    )(me, rows_in, weights)


def down_kernel(hidden_ref, weight_ref, out_ref):
    cols = out_ref.shape[1]
    span, slab = GROUP * BLOCK, GROUP * CAP
    total = mm(hidden_ref[0], weight_ref[0])
    for k in range(1, hidden_ref.shape[0]):
        total += mm(hidden_ref[k], weight_ref[k])
    total = total.astype(BF16)
    spread = regroup_matrix(True)
    for g in range(out_ref.shape[0] // span):
        block = total[g * slab : (g + 1) * slab, :]
        stacked = jnp.concatenate([block[:, q * cols : (q + 1) * cols] for q in range(QUARTERS)], axis=0)
        out_ref[g * span : (g + 1) * span, :] = mm(spread, stacked).astype(BF16)


def down(hidden, weights):
    parts, rows, units = hidden.shape
    cols = weights.shape[2] // QUARTERS
    vmem = pl.BlockSpec(memory_space=pltpu.VMEM)
    return pl.pallas_call(
        down_kernel,
        out_shape=jax.ShapeDtypeStruct((rows * QUARTERS, cols), BF16),
        in_specs=[vmem, vmem],
        out_specs=vmem,
        compiler_params=pltpu.CompilerParams(vmem_limit_bytes=24 * 1024 * 1024),
        name="down",
    )(hidden, weights)


def mixer_kernel(ids_ref, weight_ref, earlier_ref, expert_ref, slot_ref, quarter_ref, out_ref):
    rows, top = ids_ref.shape
    flight = expert_ref.shape[0]
    expert = lax.broadcasted_iota(jnp.int32, (rows, flight), 1)
    named = jnp.zeros((rows, flight), F32)
    weight = jnp.zeros((rows, flight), F32)
    for k in range(top):
        hit = ids_ref[:, k : k + 1] == expert
        named += jnp.where(hit, 1.0, 0.0)
        weight += jnp.where(hit, weight_ref[:, k : k + 1], 0.0)
    slot = mm(earlier_ref[...], named.astype(BF16))
    slot = jnp.where(named > 0, slot, FAR).astype(BF16)
    gap = mm(slot, expert_ref[...]) + mm(quarter_ref[...], slot_ref[...])
    out_ref[...] = jnp.where(gap == 0, mm(weight.astype(BF16), expert_ref[...]), 0.0).astype(BF16)


def mixer(ids, weight, flight):
    rows = ids.shape[0]
    places = flight * BLOCK
    code = place_code(flight).T
    earlier = jnp.asarray(np.tril(np.ones((rows, rows), np.float32), -1), BF16)
    expert, slot = jnp.asarray(code[:flight], BF16), jnp.asarray(code[flight:], BF16)
    quarter = jnp.asarray(quarter_code(rows).T, BF16)
    whole = lambda a: pl.BlockSpec(a.shape, lambda i: (0, 0))
    return pl.pallas_call(
        mixer_kernel,
        out_shape=jax.ShapeDtypeStruct((QUARTERS * rows, places), BF16),
        grid=(QUARTERS,),
        in_specs=[whole(ids), whole(weight), whole(earlier), whole(expert), whole(slot),
                  pl.BlockSpec((rows, 16), lambda i: (i, 0))],
        out_specs=pl.BlockSpec((rows, places), lambda i: (i, 0)),
        compiler_params=PARAMS,
        name="mixer",
    )(ids, weight, earlier, expert, slot, quarter)


def combine_kernel(mixer_ref, returned_ref, out_ref):
    rows = out_ref.shape[0]
    cols = returned_ref.shape[1]
    for q in range(QUARTERS):
        mixed = mm(mixer_ref[q * rows : (q + 1) * rows, :], returned_ref[...])
        out_ref[:, q * cols : (q + 1) * cols] = mixed.astype(BF16)


def combine(mix, returned):
    cols = returned.shape[1]
    vmem = pl.BlockSpec(memory_space=pltpu.VMEM)
    return pl.pallas_call(
        combine_kernel,
        out_shape=jax.ShapeDtypeStruct((mix.shape[0] // QUARTERS, QUARTERS * cols), BF16),
        in_specs=[vmem, vmem],
        out_specs=vmem,
        compiler_params=pltpu.CompilerParams(vmem_limit_bytes=24 * 1024 * 1024),
        name="combine",
    )(mix, returned)


def tie(*values):
    return lax.optimization_barrier(values)


def local(tokens, expert_ids, route_weight, gate_up, down_proj):
    flight = lax.axis_size("ep")
    n_tp = lax.axis_size("tp")
    features = tokens.shape[1]
    cols = features // QUARTERS
    units = gate_up.shape[2] // n_tp
    pieces = units // PIECE
    up_weights = gate_up.reshape(2, n_tp * pieces, PIECE, features)
    down_weights = down_proj.reshape(n_tp, units, features)
    me = lax.axis_index("tp").astype(jnp.int32).reshape(1)
    near = [(i, i ^ 1) for i in range(n_tp)]
    far = [(i, i ^ 2) for i in range(n_tp)]

    def pair_sum(got, keep):
        return (got.astype(F32) + keep.astype(F32)).astype(BF16)

    sent = pack(expert_ids.T, tokens, flight)
    received = lax.all_to_all(sent.reshape(flight, BLOCK, cols), "ep", 0, 0, tiled=True).reshape(flight * BLOCK, cols)

    rows, far_1, far_2 = first_part(me, 3, received, up_weights)
    got_1 = lax.ppermute(far_1, "tp", near)
    got_2 = lax.ppermute(far_2, "tp", near)
    keep_1, keep_2 = parts(me, 2, rows, up_weights, 1, pieces - 1)
    pair_1 = pair_sum(got_1, keep_1)
    rows, pair_1 = tie(rows, pair_1)
    got_1 = lax.ppermute(pair_1, "tp", far)
    (for_near,) = parts(me, 1, rows, up_weights, pieces)
    got_near = lax.ppermute(for_near, "tp", near)
    for_near, got_2 = tie(for_near, got_2)
    pair_2 = pair_sum(got_2, keep_2)
    rows, pair_2, got_1 = tie(rows, pair_2, got_1)
    got_2 = lax.ppermute(pair_2, "tp", far)
    (keep,) = parts(me, 0, rows, up_weights, pieces)
    got = [got_1] + [got_2[:, p * 2 * PIECE : (p + 1) * 2 * PIECE] for p in range(pieces - 1)]
    hidden = []
    for p in range(pieces):
        columns = slice(p * 2 * PIECE, (p + 1) * 2 * PIECE)
        summed = got[p].astype(F32) + got_near[:, columns].astype(F32) + keep[:, columns].astype(F32)
        hidden.append((jax.nn.silu(summed[:, :PIECE]) * summed[:, PIECE:]).astype(BF16))
    hidden = lax.all_gather(jnp.concatenate(hidden, axis=1), "tp", axis=0, tiled=False)

    result = down(hidden, down_weights)
    returned = lax.all_to_all(result.reshape(flight, BLOCK, cols), "ep", 0, 0, tiled=True).reshape(flight * BLOCK, cols)
    mix = mixer(expert_ids, route_weight, flight)
    return combine(mix, returned)


def solution(mesh):
    return jax.shard_map(
        local,
        mesh=mesh,
        in_specs=(
            P(("dp", "ep"), "tp"),
            P(("dp", "ep"), None),
            P(("dp", "ep"), None),
            P("ep", None, None, "tp"),
            P("ep", None, "tp"),
        ),
        out_specs=P(("dp", "ep"), "tp"),
        check_vma=False,
    )
```

```python
import functools

import jax
import jax.numpy as jnp
import numpy as np
from jax import lax
from jax.experimental import pallas as pl
from jax.experimental.pallas import tpu as pltpu
from jax.sharding import PartitionSpec as P

CAP = 10
QUARTERS = 4
FAR = 200.0
APART = 512.0
BF16 = jnp.bfloat16
F32 = jnp.float32
PARAMS = pltpu.CompilerParams(vmem_limit_bytes=48 * 1024 * 1024)
BLOCK = QUARTERS * CAP
GROUP = 8
PIECE = 128


def mm(a, b):
    return jnp.dot(a, b, preferred_element_type=F32)


def mm_t(a, b):
    return lax.dot_general(a, b, (((1,), (1,)), ((), ())), preferred_element_type=F32)


def place_code(flight):
    rows = np.arange(flight * BLOCK)
    expert, quarter, slot = rows // BLOCK, rows // CAP % QUARTERS, rows % CAP
    code = np.zeros((rows.size, flight + 16), np.float32)
    code[rows, expert] = 1
    code[:, flight] = -slot
    code[rows, flight + 1 + quarter] = APART
    return code


def quarter_code(rows):
    code = np.zeros((16, QUARTERS * rows), np.float32)
    code[0] = 1
    for quarter in range(QUARTERS):
        code[1 + quarter] = np.arange(QUARTERS * rows) // rows != quarter
    return code


def counter(shape, dim):
    return lax.broadcasted_iota(jnp.int32, shape, dim).astype(F32)


def split(number, size):
    quotient = jnp.floor((number + 0.5) * (1.0 / size))
    return quotient, number - size * quotient


def regroup_matrix(back):
    span = GROUP * BLOCK
    row = counter((span, 1), 0)
    if back:
        source, rest = split(row, BLOCK)
        quarter, slot = split(rest, CAP)
        column = quarter * (GROUP * CAP) + source * CAP + slot
    else:
        quarter, rest = split(row, GROUP * CAP)
        source, slot = split(rest, CAP)
        column = source * BLOCK + quarter * CAP + slot
    return jnp.where(counter((span, span), 1) == column, 1.0, 0.0).astype(BF16)


def pack_kernel(flight, ids_ref, token_ref, out_ref):
    top, rows = ids_ref.shape
    places, cols = out_ref.shape
    expert = lax.broadcasted_iota(jnp.int32, (flight, rows), 0)
    named = jnp.zeros((flight, rows), F32)
    for k in range(top):
        named += jnp.where(ids_ref[k : k + 1, :] == expert, 1.0, 0.0)
    earlier = jnp.where(counter((rows, rows), 0) < counter((rows, rows), 1), 1.0, 0.0).astype(BF16)
    slot = jnp.where(named > 0, mm(named.astype(BF16), earlier), FAR)

    line = counter((16, rows), 0)
    other = [jnp.where((line <= QUARTERS) & (line != q + 1), 1.0, 0.0) for q in range(QUARTERS)]
    code = jnp.concatenate([jnp.concatenate([slot, o], axis=0) for o in other], axis=1).astype(BF16)
    place = counter((places, 1), 0) + (pl.program_id(0) * places).astype(F32)
    owner, rest = split(place, BLOCK)
    quarter, place_slot = split(rest, CAP)
    column = counter((places, flight + 16), 1)
    place_code = jnp.where(column == owner, 1.0, 0.0) + jnp.where(column == flight, -place_slot, 0.0)
    place_code += jnp.where(column == flight + 1 + quarter, APART, 0.0)
    gap = mm(place_code.astype(BF16), code)
    selector = jnp.where(gap == 0, 1.0, 0.0).astype(BF16)
    stacked = jnp.concatenate([token_ref[:, q * cols : (q + 1) * cols] for q in range(QUARTERS)], axis=0)
    out_ref[...] = mm(selector, stacked).astype(BF16)


def pack(ids_t, tokens, flight):
    rows, features = tokens.shape
    places = flight * BLOCK
    steps = 2
    whole = lambda a: pl.BlockSpec(a.shape, lambda i: (0, 0))
    return pl.pallas_call(
        functools.partial(pack_kernel, flight),
        out_shape=jax.ShapeDtypeStruct((places, features // QUARTERS), BF16),
        grid=(steps,),
        in_specs=[whole(ids_t), whole(tokens)],
        out_specs=pl.BlockSpec((places // steps, features // QUARTERS), lambda i: (i, 0)),
        compiler_params=pltpu.CompilerParams(vmem_limit_bytes=60 * 1024 * 1024),
        name="pack",
    )(ids_t, tokens)


def first_kernel(x_ref, weight_ref, rows_ref, first_ref, rest_ref):
    cols = x_ref.shape[1]
    span, slab = GROUP * BLOCK, GROUP * CAP
    regroup = regroup_matrix(False)
    for g in range(x_ref.shape[0] // span):
        sorted_rows = mm(regroup, x_ref[g * span : (g + 1) * span, :]).astype(BF16)
        for q in range(QUARTERS):
            rows_ref[g * slab : (g + 1) * slab, q * cols : (q + 1) * cols] = sorted_rows[q * slab : (q + 1) * slab]
    for piece in range(weight_ref.shape[1]):
        product = mm_t(rows_ref[...], weight_ref[:, piece].reshape(2 * PIECE, -1)).astype(BF16)
        if piece == 0:
            first_ref[...] = product
        else:
            rest_ref[:, (piece - 1) * 2 * PIECE : piece * 2 * PIECE] = product


def piece_of(weights, quarter, mask, piece):
    return (quarter ^ mask) * (weights.shape[1] // QUARTERS) + piece


def first_part(received, weights):
    places, cols = received.shape
    rows, features = places // QUARTERS, QUARTERS * cols
    pieces = weights.shape[1]
    shapes = [(rows, features), (rows, 2 * PIECE), (rows, 2 * PIECE * (pieces - 1))]
    vmem = pl.BlockSpec(memory_space=pltpu.VMEM)
    return pl.pallas_call(
        first_kernel,
        out_shape=tuple(jax.ShapeDtypeStruct(shape, BF16) for shape in shapes),
        in_specs=[vmem, vmem],
        out_specs=(vmem,) * 3,
        compiler_params=pltpu.CompilerParams(vmem_limit_bytes=24 * 1024 * 1024),
        cost_estimate=pl.CostEstimate(flops=2 * rows * weights.size, bytes_accessed=2 * weights.size, transcendentals=0),
        name="first",
    )(received, weights)


def parts_kernel(pieces, me_ref, rows_ref, weight_ref, *out_refs):
    steps = [(out_ref, p) for out_ref, count in zip(out_refs, pieces) for p in range(count)]
    for i, (out_ref, p) in enumerate(steps):
        @pl.when(pl.program_id(0) == i)
        def _():
            product = mm_t(rows_ref[...], weight_ref[...].reshape(2 * PIECE, -1))
            out_ref[:, p * 2 * PIECE : (p + 1) * 2 * PIECE] = product.astype(BF16)


def parts(me, mask, rows_in, weights, *pieces, start=0):
    rows, features = rows_in.shape
    steps = sum(pieces)
    whole = lambda shape: pl.BlockSpec(shape, lambda i, me: (0, 0))
    shapes = [(rows, 2 * PIECE * count) for count in pieces]
    return pl.pallas_call(
        functools.partial(parts_kernel, pieces),
        out_shape=tuple(jax.ShapeDtypeStruct(shape, BF16) for shape in shapes),
        grid_spec=pltpu.PrefetchScalarGridSpec(
            num_scalar_prefetch=1,
            grid=(steps,),
            in_specs=[whole((rows, features)),
                      pl.BlockSpec((2, 1, PIECE, features), lambda i, me: (0, piece_of(weights, me[0], mask, start + i), 0, 0))],
            out_specs=tuple(whole(shape) for shape in shapes),
        ),
        compiler_params=PARAMS,
        cost_estimate=pl.CostEstimate(flops=4 * steps * rows * PIECE * features, bytes_accessed=4 * steps * PIECE * features, transcendentals=0),
        name="parts",
    )(me, rows_in, weights)


def down_kernel(hidden_ref, weight_ref, out_ref):
    cols = out_ref.shape[1]
    span, slab = GROUP * BLOCK, GROUP * CAP
    hidden = jnp.concatenate([hidden_ref[k] for k in range(hidden_ref.shape[0])], axis=1)
    total = mm(hidden, weight_ref[...]).astype(BF16)
    spread = regroup_matrix(True)
    for g in range(out_ref.shape[0] // span):
        block = total[g * slab : (g + 1) * slab, :]
        stacked = jnp.concatenate([block[:, q * cols : (q + 1) * cols] for q in range(QUARTERS)], axis=0)
        out_ref[g * span : (g + 1) * span, :] = mm(spread, stacked).astype(BF16)


def down(hidden, weights):
    parts, rows, units = hidden.shape
    cols = weights.shape[1] // QUARTERS
    vmem = pl.BlockSpec(memory_space=pltpu.VMEM)
    return pl.pallas_call(
        down_kernel,
        out_shape=jax.ShapeDtypeStruct((rows * QUARTERS, cols), BF16),
        in_specs=[vmem, vmem],
        out_specs=vmem,
        compiler_params=pltpu.CompilerParams(vmem_limit_bytes=24 * 1024 * 1024),
        name="down",
    )(hidden, weights)


def mixer_kernel(ids_ref, weight_ref, earlier_ref, expert_ref, slot_ref, quarter_ref, out_ref):
    rows, top = ids_ref.shape
    flight = expert_ref.shape[0]
    expert = lax.broadcasted_iota(jnp.int32, (rows, flight), 1)
    named = jnp.zeros((rows, flight), F32)
    weight = jnp.zeros((rows, flight), F32)
    for k in range(top):
        hit = ids_ref[:, k : k + 1] == expert
        named += jnp.where(hit, 1.0, 0.0)
        weight += jnp.where(hit, weight_ref[:, k : k + 1], 0.0)
    slot = mm(earlier_ref[...], named.astype(BF16))
    slot = jnp.where(named > 0, slot, FAR).astype(BF16)
    gap = mm(slot, expert_ref[...]) + mm(quarter_ref[...], slot_ref[...])
    out_ref[...] = jnp.where(gap == 0, mm(weight.astype(BF16), expert_ref[...]), 0.0).astype(BF16)


def mixer(ids, weight, flight):
    rows = ids.shape[0]
    places = flight * BLOCK
    code = place_code(flight).T
    earlier = jnp.asarray(np.tril(np.ones((rows, rows), np.float32), -1), BF16)
    expert, slot = jnp.asarray(code[:flight], BF16), jnp.asarray(code[flight:], BF16)
    quarter = jnp.asarray(quarter_code(rows).T, BF16)
    whole = lambda a: pl.BlockSpec(a.shape, lambda i: (0, 0))
    return pl.pallas_call(
        mixer_kernel,
        out_shape=jax.ShapeDtypeStruct((QUARTERS * rows, places), BF16),
        grid=(QUARTERS,),
        in_specs=[whole(ids), whole(weight), whole(earlier), whole(expert), whole(slot),
                  pl.BlockSpec((rows, 16), lambda i: (i, 0))],
        out_specs=pl.BlockSpec((rows, places), lambda i: (i, 0)),
        compiler_params=PARAMS,
        name="mixer",
    )(ids, weight, earlier, expert, slot, quarter)


def combine_kernel(mixer_ref, returned_ref, out_ref):
    rows = out_ref.shape[0]
    cols = returned_ref.shape[1]
    for q in range(QUARTERS):
        mixed = mm(mixer_ref[q * rows : (q + 1) * rows, :], returned_ref[...])
        out_ref[:, q * cols : (q + 1) * cols] = mixed.astype(BF16)


def combine(mix, returned):
    cols = returned.shape[1]
    vmem = pl.BlockSpec(memory_space=pltpu.VMEM)
    return pl.pallas_call(
        combine_kernel,
        out_shape=jax.ShapeDtypeStruct((mix.shape[0] // QUARTERS, QUARTERS * cols), BF16),
        in_specs=[vmem, vmem],
        out_specs=vmem,
        compiler_params=pltpu.CompilerParams(vmem_limit_bytes=24 * 1024 * 1024),
        name="combine",
    )(mix, returned)


def tie(*values):
    return lax.optimization_barrier(values)


def local(tokens, expert_ids, route_weight, gate_up, down_proj):
    flight = lax.axis_size("ep")
    n_tp = lax.axis_size("tp")
    features = tokens.shape[1]
    cols = features // QUARTERS
    units = gate_up.shape[2] // n_tp
    pieces = units // PIECE
    up_weights = gate_up.reshape(2, n_tp * pieces, PIECE, features)
    me = lax.axis_index("tp").astype(jnp.int32).reshape(1)
    near = [(i, i ^ 1) for i in range(n_tp)]
    far = [(i, i ^ 2) for i in range(n_tp)]

    def pair_sum(got, keep):
        return (got.astype(F32) + keep.astype(F32)).astype(BF16)

    sent = pack(expert_ids.T, tokens, flight)
    sent, up_weights = tie(sent, up_weights)
    first_weights = lax.dynamic_slice_in_dim(up_weights, (me[0] ^ 3) * pieces, pieces, axis=1)
    received = lax.all_to_all(sent.reshape(flight, BLOCK, cols), "ep", 0, 0, tiled=True).reshape(flight * BLOCK, cols)

    rows, far_1, far_2 = first_part(received, first_weights)
    got_1 = lax.ppermute(far_1, "tp", near)
    got_2 = lax.ppermute(far_2, "tp", near)
    keep_1, keep_2 = parts(me, 2, rows, up_weights, 1, pieces - 1)
    pair_1 = pair_sum(got_1, keep_1)
    rows, pair_1 = tie(rows, pair_1)
    got_1 = lax.ppermute(pair_1, "tp", far)
    (for_near,) = parts(me, 1, rows, up_weights, pieces)
    got_near = lax.ppermute(for_near, "tp", near)
    for_near, got_2 = tie(for_near, got_2)
    pair_2 = pair_sum(got_2, keep_2)
    rows, pair_2, got_1 = tie(rows, pair_2, got_1)
    got_2 = lax.ppermute(pair_2, "tp", far)
    (keep,) = parts(me, 0, rows, up_weights, pieces)
    got = [got_1] + [got_2[:, p * 2 * PIECE : (p + 1) * 2 * PIECE] for p in range(pieces - 1)]
    hidden = []
    for p in range(pieces):
        columns = slice(p * 2 * PIECE, (p + 1) * 2 * PIECE)
        summed = got[p].astype(F32) + got_near[:, columns].astype(F32) + keep[:, columns].astype(F32)
        hidden.append((jax.nn.silu(summed[:, :PIECE]) * summed[:, PIECE:]).astype(BF16))
    hidden = lax.all_gather(jnp.concatenate(hidden, axis=1), "tp", axis=0, tiled=False)

    result = down(hidden, down_proj[0])
    returned = lax.all_to_all(result.reshape(flight, BLOCK, cols), "ep", 0, 0, tiled=True).reshape(flight * BLOCK, cols)
    mix = mixer(expert_ids, route_weight, flight)
    return combine(mix, returned)


def solution(mesh):
    return jax.shard_map(
        local,
        mesh=mesh,
        in_specs=(
            P(("dp", "ep"), "tp"),
            P(("dp", "ep"), None),
            P(("dp", "ep"), None),
            P("ep", None, None, "tp"),
            P("ep", None, "tp"),
        ),
        out_specs=P(("dp", "ep"), "tp"),
        check_vma=False,
    )
```

```python
import functools

import jax
import jax.numpy as jnp
import numpy as np
from jax import lax
from jax.experimental import pallas as pl
from jax.experimental.pallas import tpu as pltpu
from jax.sharding import PartitionSpec as P

CAP = 10
QUARTERS = 4
FAR = 200.0
APART = 512.0
BF16 = jnp.bfloat16
F32 = jnp.float32
PARAMS = pltpu.CompilerParams(vmem_limit_bytes=48 * 1024 * 1024)
BLOCK = QUARTERS * CAP
GROUP = 8
PIECE = 128


def mm(a, b):
    return jnp.dot(a, b, preferred_element_type=F32)


def mm_t(a, b):
    return lax.dot_general(a, b, (((1,), (1,)), ((), ())), preferred_element_type=F32)


def place_code(flight):
    rows = np.arange(flight * BLOCK)
    expert, quarter, slot = rows // BLOCK, rows // CAP % QUARTERS, rows % CAP
    code = np.zeros((rows.size, flight + 16), np.float32)
    code[rows, expert] = 1
    code[:, flight] = -slot
    code[rows, flight + 1 + quarter] = APART
    return code


def quarter_code(rows):
    code = np.zeros((16, QUARTERS * rows), np.float32)
    code[0] = 1
    for quarter in range(QUARTERS):
        code[1 + quarter] = np.arange(QUARTERS * rows) // rows != quarter
    return code


def counter(shape, dim):
    return lax.broadcasted_iota(jnp.int32, shape, dim).astype(F32)


def split(number, size):
    quotient = jnp.floor((number + 0.5) * (1.0 / size))
    return quotient, number - size * quotient


def regroup_matrix(back):
    span = GROUP * BLOCK
    row = counter((span, 1), 0)
    if back:
        source, rest = split(row, BLOCK)
        quarter, slot = split(rest, CAP)
        column = quarter * (GROUP * CAP) + source * CAP + slot
    else:
        quarter, rest = split(row, GROUP * CAP)
        source, slot = split(rest, CAP)
        column = source * BLOCK + quarter * CAP + slot
    return jnp.where(counter((span, span), 1) == column, 1.0, 0.0).astype(BF16)


def pack_kernel(flight, ids_ref, token_ref, out_ref):
    top, rows = ids_ref.shape
    places, cols = out_ref.shape
    expert = lax.broadcasted_iota(jnp.int32, (flight, rows), 0)
    named = jnp.zeros((flight, rows), F32)
    for k in range(top):
        named += jnp.where(ids_ref[k : k + 1, :] == expert, 1.0, 0.0)
    earlier = jnp.where(counter((rows, rows), 0) < counter((rows, rows), 1), 1.0, 0.0).astype(BF16)
    slot = jnp.where(named > 0, mm(named.astype(BF16), earlier), FAR)

    line = counter((16, rows), 0)
    other = [jnp.where((line <= QUARTERS) & (line != q + 1), 1.0, 0.0) for q in range(QUARTERS)]
    code = jnp.concatenate([jnp.concatenate([slot, o], axis=0) for o in other], axis=1).astype(BF16)
    place = counter((places, 1), 0) + (pl.program_id(0) * places).astype(F32)
    owner, rest = split(place, BLOCK)
    quarter, place_slot = split(rest, CAP)
    column = counter((places, flight + 16), 1)
    place_code = jnp.where(column == owner, 1.0, 0.0) + jnp.where(column == flight, -place_slot, 0.0)
    place_code += jnp.where(column == flight + 1 + quarter, APART, 0.0)
    gap = mm(place_code.astype(BF16), code)
    selector = jnp.where(gap == 0, 1.0, 0.0).astype(BF16)
    stacked = jnp.concatenate([token_ref[:, q * cols : (q + 1) * cols] for q in range(QUARTERS)], axis=0)
    out_ref[...] = mm(selector, stacked).astype(BF16)


def pack(ids_t, tokens, flight):
    rows, features = tokens.shape
    places = flight * BLOCK
    steps = 1
    whole = lambda a: pl.BlockSpec(a.shape, lambda i: (0, 0))
    return pl.pallas_call(
        functools.partial(pack_kernel, flight),
        out_shape=jax.ShapeDtypeStruct((places, features // QUARTERS), BF16),
        grid=(steps,),
        in_specs=[whole(ids_t), whole(tokens)],
        out_specs=pl.BlockSpec((places // steps, features // QUARTERS), lambda i: (i, 0)),
        compiler_params=pltpu.CompilerParams(vmem_limit_bytes=60 * 1024 * 1024),
        name="pack",
    )(ids_t, tokens)


def first_kernel(x_ref, weight_ref, rows_ref, first_ref, rest_ref):
    cols = x_ref.shape[1]
    span, slab = GROUP * BLOCK, GROUP * CAP
    regroup = regroup_matrix(False)
    for g in range(x_ref.shape[0] // span):
        sorted_rows = mm(regroup, x_ref[g * span : (g + 1) * span, :]).astype(BF16)
        for q in range(QUARTERS):
            rows_ref[g * slab : (g + 1) * slab, q * cols : (q + 1) * cols] = sorted_rows[q * slab : (q + 1) * slab]
    for piece in range(weight_ref.shape[1]):
        product = mm_t(rows_ref[...], weight_ref[:, piece].reshape(2 * PIECE, -1)).astype(BF16)
        if piece == 0:
            first_ref[...] = product
        else:
            rest_ref[:, (piece - 1) * 2 * PIECE : piece * 2 * PIECE] = product


def first_part(received, weights):
    places, cols = received.shape
    rows, features = places // QUARTERS, QUARTERS * cols
    pieces = weights.shape[1]
    shapes = [(rows, features), (rows, 2 * PIECE), (rows, 2 * PIECE * (pieces - 1))]
    vmem = pl.BlockSpec(memory_space=pltpu.VMEM)
    return pl.pallas_call(
        first_kernel,
        out_shape=tuple(jax.ShapeDtypeStruct(shape, BF16) for shape in shapes),
        in_specs=[vmem, vmem],
        out_specs=(vmem,) * 3,
        compiler_params=pltpu.CompilerParams(vmem_limit_bytes=24 * 1024 * 1024),
        cost_estimate=pl.CostEstimate(flops=2 * rows * weights.size, bytes_accessed=2 * weights.size, transcendentals=0),
        name="first",
    )(received, weights)


def parts_kernel(mask, me_ref, rows_ref, weight_ref, *refs):
    *out_refs, held, arrived = refs
    pieces = held.shape[1]
    base = (me_ref[0] ^ mask) * pieces
    copies = [
        pltpu.make_async_copy(weight_ref.at[:, pl.ds(base + p, 1)], held.at[:, pl.ds(p, 1)], arrived.at[p])
        for p in range(pieces)
    ]
    for copy in copies:
        copy.start()
    piece = 0
    for out_ref in out_refs:
        for p in range(out_ref.shape[1] // (2 * PIECE)):
            copies[piece].wait()
            product = mm_t(rows_ref[...], held[:, piece].reshape(2 * PIECE, -1))
            out_ref[:, p * 2 * PIECE : (p + 1) * 2 * PIECE] = product.astype(BF16)
            piece += 1


def parts(me, mask, rows_in, weights, *pieces):
    rows, features = rows_in.shape
    count = sum(pieces)
    shapes = [(rows, 2 * PIECE * number) for number in pieces]
    vmem = pl.BlockSpec(memory_space=pltpu.VMEM)
    return pl.pallas_call(
        functools.partial(parts_kernel, mask),
        out_shape=tuple(jax.ShapeDtypeStruct(shape, BF16) for shape in shapes),
        in_specs=[pl.BlockSpec(memory_space=pltpu.SMEM), vmem, pl.BlockSpec(memory_space=pl.ANY)],
        out_specs=(vmem,) * len(shapes),
        scratch_shapes=[pltpu.VMEM((2, count, PIECE, features), BF16), pltpu.SemaphoreType.DMA((count,))],
        compiler_params=PARAMS,
        cost_estimate=pl.CostEstimate(flops=4 * count * rows * PIECE * features, bytes_accessed=4 * count * PIECE * features, transcendentals=0),
        name="parts",
    )(me, rows_in, weights)


def down_kernel(hidden_ref, weight_ref, out_ref):
    cols = out_ref.shape[1]
    span, slab = GROUP * BLOCK, GROUP * CAP
    hidden = jnp.concatenate([hidden_ref[k] for k in range(hidden_ref.shape[0])], axis=1)
    total = mm(hidden, weight_ref[...]).astype(BF16)
    spread = regroup_matrix(True)
    for g in range(out_ref.shape[0] // span):
        block = total[g * slab : (g + 1) * slab, :]
        stacked = jnp.concatenate([block[:, q * cols : (q + 1) * cols] for q in range(QUARTERS)], axis=0)
        out_ref[g * span : (g + 1) * span, :] = mm(spread, stacked).astype(BF16)


def down(hidden, weights):
    parts, rows, units = hidden.shape
    cols = weights.shape[1] // QUARTERS
    vmem = pl.BlockSpec(memory_space=pltpu.VMEM)
    return pl.pallas_call(
        down_kernel,
        out_shape=jax.ShapeDtypeStruct((rows * QUARTERS, cols), BF16),
        in_specs=[vmem, vmem],
        out_specs=vmem,
        compiler_params=pltpu.CompilerParams(vmem_limit_bytes=24 * 1024 * 1024),
        name="down",
    )(hidden, weights)


def mixer_kernel(ids_ref, weight_ref, earlier_ref, expert_ref, slot_ref, quarter_ref, out_ref):
    rows, top = ids_ref.shape
    flight = expert_ref.shape[0]
    expert = lax.broadcasted_iota(jnp.int32, (rows, flight), 1)
    named = jnp.zeros((rows, flight), F32)
    weight = jnp.zeros((rows, flight), F32)
    for k in range(top):
        hit = ids_ref[:, k : k + 1] == expert
        named += jnp.where(hit, 1.0, 0.0)
        weight += jnp.where(hit, weight_ref[:, k : k + 1], 0.0)
    slot = mm(earlier_ref[...], named.astype(BF16))
    slot = jnp.where(named > 0, slot, FAR).astype(BF16)
    gap = mm(slot, expert_ref[...]) + mm(quarter_ref[...], slot_ref[...])
    out_ref[...] = jnp.where(gap == 0, mm(weight.astype(BF16), expert_ref[...]), 0.0).astype(BF16)


def mixer(ids, weight, flight):
    rows = ids.shape[0]
    places = flight * BLOCK
    code = place_code(flight).T
    earlier = jnp.asarray(np.tril(np.ones((rows, rows), np.float32), -1), BF16)
    expert, slot = jnp.asarray(code[:flight], BF16), jnp.asarray(code[flight:], BF16)
    quarter = jnp.asarray(quarter_code(rows).T, BF16)
    whole = lambda a: pl.BlockSpec(a.shape, lambda i: (0, 0))
    return pl.pallas_call(
        mixer_kernel,
        out_shape=jax.ShapeDtypeStruct((QUARTERS * rows, places), BF16),
        grid=(QUARTERS,),
        in_specs=[whole(ids), whole(weight), whole(earlier), whole(expert), whole(slot),
                  pl.BlockSpec((rows, 16), lambda i: (i, 0))],
        out_specs=pl.BlockSpec((rows, places), lambda i: (i, 0)),
        compiler_params=PARAMS,
        name="mixer",
    )(ids, weight, earlier, expert, slot, quarter)


def combine_kernel(mixer_ref, returned_ref, out_ref):
    rows = out_ref.shape[0]
    cols = returned_ref.shape[1]
    for q in range(QUARTERS):
        mixed = mm(mixer_ref[q * rows : (q + 1) * rows, :], returned_ref[...])
        out_ref[:, q * cols : (q + 1) * cols] = mixed.astype(BF16)


def combine(mix, returned):
    cols = returned.shape[1]
    vmem = pl.BlockSpec(memory_space=pltpu.VMEM)
    return pl.pallas_call(
        combine_kernel,
        out_shape=jax.ShapeDtypeStruct((mix.shape[0] // QUARTERS, QUARTERS * cols), BF16),
        in_specs=[vmem, vmem],
        out_specs=vmem,
        compiler_params=pltpu.CompilerParams(vmem_limit_bytes=24 * 1024 * 1024),
        name="combine",
    )(mix, returned)


def tie(*values):
    return lax.optimization_barrier(values)


def local(tokens, expert_ids, route_weight, gate_up, down_proj):
    flight = lax.axis_size("ep")
    n_tp = lax.axis_size("tp")
    features = tokens.shape[1]
    cols = features // QUARTERS
    units = gate_up.shape[2] // n_tp
    pieces = units // PIECE
    up_weights = gate_up.reshape(2, n_tp * pieces, PIECE, features)
    me = lax.axis_index("tp").astype(jnp.int32).reshape(1)
    near = [(i, i ^ 1) for i in range(n_tp)]
    far = [(i, i ^ 2) for i in range(n_tp)]

    def pair_sum(got, keep):
        return (got.astype(F32) + keep.astype(F32)).astype(BF16)

    sent = pack(expert_ids.T, tokens, flight)
    sent, up_weights = tie(sent, up_weights)
    first_weights = lax.dynamic_slice_in_dim(up_weights, (me[0] ^ 3) * pieces, pieces, axis=1)
    received = lax.all_to_all(sent.reshape(flight, BLOCK, cols), "ep", 0, 0, tiled=True).reshape(flight * BLOCK, cols)

    rows, far_1, far_2 = first_part(received, first_weights)
    got_1 = lax.ppermute(far_1, "tp", near)
    got_2 = lax.ppermute(far_2, "tp", near)
    keep_1, keep_2 = parts(me, 2, rows, up_weights, 1, pieces - 1)
    pair_1 = pair_sum(got_1, keep_1)
    rows, pair_1 = tie(rows, pair_1)
    got_1 = lax.ppermute(pair_1, "tp", far)
    (for_near,) = parts(me, 1, rows, up_weights, pieces)
    got_near = lax.ppermute(for_near, "tp", near)
    for_near, got_2 = tie(for_near, got_2)
    pair_2 = pair_sum(got_2, keep_2)
    rows, pair_2, got_1 = tie(rows, pair_2, got_1)
    got_2 = lax.ppermute(pair_2, "tp", far)
    (keep,) = parts(me, 0, rows, up_weights, pieces)
    got = [got_1] + [got_2[:, p * 2 * PIECE : (p + 1) * 2 * PIECE] for p in range(pieces - 1)]
    hidden = []
    for p in range(pieces):
        columns = slice(p * 2 * PIECE, (p + 1) * 2 * PIECE)
        summed = got[p].astype(F32) + got_near[:, columns].astype(F32) + keep[:, columns].astype(F32)
        hidden.append((jax.nn.silu(summed[:, :PIECE]) * summed[:, PIECE:]).astype(BF16))
    hidden = lax.all_gather(jnp.concatenate(hidden, axis=1), "tp", axis=0, tiled=False)

    result = down(hidden, down_proj[0])
    returned = lax.all_to_all(result.reshape(flight, BLOCK, cols), "ep", 0, 0, tiled=True).reshape(flight * BLOCK, cols)
    mix = mixer(expert_ids, route_weight, flight)
    return combine(mix, returned)


def solution(mesh):
    return jax.shard_map(
        local,
        mesh=mesh,
        in_specs=(
            P(("dp", "ep"), "tp"),
            P(("dp", "ep"), None),
            P(("dp", "ep"), None),
            P("ep", None, None, "tp"),
            P("ep", None, "tp"),
        ),
        out_specs=P(("dp", "ep"), "tp"),
        check_vma=False,
    )
```

```python
import functools

import jax
import jax.numpy as jnp
import numpy as np
from jax import lax
from jax.experimental import pallas as pl
from jax.experimental.pallas import tpu as pltpu
from jax.sharding import PartitionSpec as P

CAP = 10
QUARTERS = 4
FAR = 200.0
APART = 512.0
BF16 = jnp.bfloat16
F32 = jnp.float32
PARAMS = pltpu.CompilerParams(vmem_limit_bytes=48 * 1024 * 1024)
BLOCK = QUARTERS * CAP
GROUP = 8
PIECE = 128


def mm(a, b):
    return jnp.dot(a, b, preferred_element_type=F32)


def mm_t(a, b):
    return lax.dot_general(a, b, (((1,), (1,)), ((), ())), preferred_element_type=F32)


def place_code(flight):
    rows = np.arange(flight * BLOCK)
    expert, quarter, slot = rows // BLOCK, rows // CAP % QUARTERS, rows % CAP
    code = np.zeros((rows.size, flight + 16), np.float32)
    code[rows, expert] = 1
    code[:, flight] = -slot
    code[rows, flight + 1 + quarter] = APART
    return code


def quarter_code(rows):
    code = np.zeros((16, QUARTERS * rows), np.float32)
    code[0] = 1
    for quarter in range(QUARTERS):
        code[1 + quarter] = np.arange(QUARTERS * rows) // rows != quarter
    return code


def counter(shape, dim):
    return lax.broadcasted_iota(jnp.int32, shape, dim).astype(F32)


def split(number, size):
    quotient = jnp.floor((number + 0.5) * (1.0 / size))
    return quotient, number - size * quotient


def regroup_matrix(back):
    span = GROUP * BLOCK
    row = counter((span, 1), 0)
    if back:
        source, rest = split(row, BLOCK)
        quarter, slot = split(rest, CAP)
        column = quarter * (GROUP * CAP) + source * CAP + slot
    else:
        quarter, rest = split(row, GROUP * CAP)
        source, slot = split(rest, CAP)
        column = source * BLOCK + quarter * CAP + slot
    return jnp.where(counter((span, span), 1) == column, 1.0, 0.0).astype(BF16)


def spread(rows, out_ref):
    cols = out_ref.shape[1]
    span, slab = GROUP * BLOCK, GROUP * CAP
    matrix = regroup_matrix(True)
    for g in range(out_ref.shape[0] // span):
        block = rows[g * slab : (g + 1) * slab, :]
        stacked = jnp.concatenate([block[:, q * cols : (q + 1) * cols] for q in range(QUARTERS)], axis=0)
        out_ref[g * span : (g + 1) * span, :] = mm(matrix, stacked).astype(BF16)


def pack_kernel(flight, ids_ref, token_ref, out_ref):
    top, rows = ids_ref.shape
    expert = lax.broadcasted_iota(jnp.int32, (flight, rows), 0)
    named = jnp.zeros((flight, rows), F32)
    for k in range(top):
        named += jnp.where(ids_ref[k : k + 1, :] == expert, 1.0, 0.0)
    earlier = jnp.where(counter((rows, rows), 0) < counter((rows, rows), 1), 1.0, 0.0).astype(BF16)
    slot = jnp.where(named > 0, mm(named.astype(BF16), earlier), FAR)

    ones = jnp.where(counter((16, rows), 0) == 0, 1.0, 0.0)
    code = jnp.concatenate([slot, ones], axis=0).astype(BF16)
    places = flight * CAP
    owner, place_slot = split(counter((places, 1), 0), CAP)
    column = counter((places, flight + 16), 1)
    place_code = jnp.where(column == owner, 1.0, 0.0) + jnp.where(column == flight, -place_slot, 0.0)
    gap = mm(place_code.astype(BF16), code)
    selector = jnp.where(gap == 0, 1.0, 0.0).astype(BF16)
    spread(mm(selector, token_ref[...]).astype(BF16), out_ref)


def pack(ids_t, tokens, flight):
    features = tokens.shape[1]
    whole = lambda shape: pl.BlockSpec(shape, lambda i: (0, 0))
    shape = (flight * BLOCK, features // QUARTERS)
    return pl.pallas_call(
        functools.partial(pack_kernel, flight),
        out_shape=jax.ShapeDtypeStruct(shape, BF16),
        grid=(1,),
        in_specs=[whole(ids_t.shape), whole(tokens.shape)],
        out_specs=whole(shape),
        compiler_params=pltpu.CompilerParams(vmem_limit_bytes=60 * 1024 * 1024),
        name="pack",
    )(ids_t, tokens)


def first_kernel(x_ref, weight_ref, rows_ref, first_ref, rest_ref):
    cols = x_ref.shape[1]
    span, slab = GROUP * BLOCK, GROUP * CAP
    regroup = regroup_matrix(False)
    for g in range(x_ref.shape[0] // span):
        sorted_rows = mm(regroup, x_ref[g * span : (g + 1) * span, :]).astype(BF16)
        for q in range(QUARTERS):
            rows_ref[g * slab : (g + 1) * slab, q * cols : (q + 1) * cols] = sorted_rows[q * slab : (q + 1) * slab]
    for piece in range(weight_ref.shape[1]):
        product = mm_t(rows_ref[...], weight_ref[:, piece].reshape(2 * PIECE, -1)).astype(BF16)
        if piece == 0:
            first_ref[...] = product
        else:
            rest_ref[:, (piece - 1) * 2 * PIECE : piece * 2 * PIECE] = product


def first_part(received, weights):
    places, cols = received.shape
    rows, features = places // QUARTERS, QUARTERS * cols
    pieces = weights.shape[1]
    shapes = [(rows, features), (rows, 2 * PIECE), (rows, 2 * PIECE * (pieces - 1))]
    vmem = pl.BlockSpec(memory_space=pltpu.VMEM)
    return pl.pallas_call(
        first_kernel,
        out_shape=tuple(jax.ShapeDtypeStruct(shape, BF16) for shape in shapes),
        in_specs=[vmem, vmem],
        out_specs=(vmem,) * 3,
        compiler_params=pltpu.CompilerParams(vmem_limit_bytes=24 * 1024 * 1024),
        cost_estimate=pl.CostEstimate(flops=2 * rows * weights.size, bytes_accessed=2 * weights.size, transcendentals=0),
        name="first",
    )(received, weights)


def parts_kernel(mask, me_ref, rows_ref, weight_ref, *refs):
    *out_refs, held, arrived = refs
    pieces = held.shape[1]
    base = (me_ref[0] ^ mask) * pieces
    copies = [
        pltpu.make_async_copy(weight_ref.at[:, pl.ds(base + p, 1)], held.at[:, pl.ds(p, 1)], arrived.at[p])
        for p in range(pieces)
    ]
    for copy in copies:
        copy.start()
    piece = 0
    for out_ref in out_refs:
        for p in range(out_ref.shape[1] // (2 * PIECE)):
            copies[piece].wait()
            product = mm_t(rows_ref[...], held[:, piece].reshape(2 * PIECE, -1))
            out_ref[:, p * 2 * PIECE : (p + 1) * 2 * PIECE] = product.astype(BF16)
            piece += 1


def parts(me, mask, rows_in, weights, *pieces):
    rows, features = rows_in.shape
    count = sum(pieces)
    shapes = [(rows, 2 * PIECE * number) for number in pieces]
    vmem = pl.BlockSpec(memory_space=pltpu.VMEM)
    return pl.pallas_call(
        functools.partial(parts_kernel, mask),
        out_shape=tuple(jax.ShapeDtypeStruct(shape, BF16) for shape in shapes),
        in_specs=[pl.BlockSpec(memory_space=pltpu.SMEM), vmem, pl.BlockSpec(memory_space=pl.ANY)],
        out_specs=(vmem,) * len(shapes),
        scratch_shapes=[pltpu.VMEM((2, count, PIECE, features), BF16), pltpu.SemaphoreType.DMA((count,))],
        compiler_params=PARAMS,
        cost_estimate=pl.CostEstimate(flops=4 * count * rows * PIECE * features, bytes_accessed=4 * count * PIECE * features, transcendentals=0),
        name="parts",
    )(me, rows_in, weights)


def down_kernel(hidden_ref, weight_ref, out_ref):
    hidden = jnp.concatenate([hidden_ref[k] for k in range(hidden_ref.shape[0])], axis=1)
    spread(mm(hidden, weight_ref[...]).astype(BF16), out_ref)


def down(hidden, weights):
    parts, rows, units = hidden.shape
    cols = weights.shape[1] // QUARTERS
    vmem = pl.BlockSpec(memory_space=pltpu.VMEM)
    return pl.pallas_call(
        down_kernel,
        out_shape=jax.ShapeDtypeStruct((rows * QUARTERS, cols), BF16),
        in_specs=[vmem, vmem],
        out_specs=vmem,
        compiler_params=pltpu.CompilerParams(vmem_limit_bytes=24 * 1024 * 1024),
        name="down",
    )(hidden, weights)


def mixer_kernel(ids_ref, weight_ref, earlier_ref, expert_ref, slot_ref, quarter_ref, out_ref):
    rows, top = ids_ref.shape
    flight = expert_ref.shape[0]
    expert = lax.broadcasted_iota(jnp.int32, (rows, flight), 1)
    named = jnp.zeros((rows, flight), F32)
    weight = jnp.zeros((rows, flight), F32)
    for k in range(top):
        hit = ids_ref[:, k : k + 1] == expert
        named += jnp.where(hit, 1.0, 0.0)
        weight += jnp.where(hit, weight_ref[:, k : k + 1], 0.0)
    slot = mm(earlier_ref[...], named.astype(BF16))
    slot = jnp.where(named > 0, slot, FAR).astype(BF16)
    gap = mm(slot, expert_ref[...]) + mm(quarter_ref[...], slot_ref[...])
    out_ref[...] = jnp.where(gap == 0, mm(weight.astype(BF16), expert_ref[...]), 0.0).astype(BF16)


def mixer(ids, weight, flight):
    rows = ids.shape[0]
    places = flight * BLOCK
    code = place_code(flight).T
    earlier = jnp.asarray(np.tril(np.ones((rows, rows), np.float32), -1), BF16)
    expert, slot = jnp.asarray(code[:flight], BF16), jnp.asarray(code[flight:], BF16)
    quarter = jnp.asarray(quarter_code(rows).T, BF16)
    whole = lambda a: pl.BlockSpec(a.shape, lambda i: (0, 0))
    return pl.pallas_call(
        mixer_kernel,
        out_shape=jax.ShapeDtypeStruct((QUARTERS * rows, places), BF16),
        grid=(QUARTERS,),
        in_specs=[whole(ids), whole(weight), whole(earlier), whole(expert), whole(slot),
                  pl.BlockSpec((rows, 16), lambda i: (i, 0))],
        out_specs=pl.BlockSpec((rows, places), lambda i: (i, 0)),
        compiler_params=PARAMS,
        name="mixer",
    )(ids, weight, earlier, expert, slot, quarter)


def combine_kernel(mixer_ref, returned_ref, out_ref):
    rows = out_ref.shape[0]
    cols = returned_ref.shape[1]
    for q in range(QUARTERS):
        mixed = mm(mixer_ref[q * rows : (q + 1) * rows, :], returned_ref[...])
        out_ref[:, q * cols : (q + 1) * cols] = mixed.astype(BF16)


def combine(mix, returned):
    cols = returned.shape[1]
    vmem = pl.BlockSpec(memory_space=pltpu.VMEM)
    return pl.pallas_call(
        combine_kernel,
        out_shape=jax.ShapeDtypeStruct((mix.shape[0] // QUARTERS, QUARTERS * cols), BF16),
        in_specs=[vmem, vmem],
        out_specs=vmem,
        compiler_params=pltpu.CompilerParams(vmem_limit_bytes=24 * 1024 * 1024),
        name="combine",
    )(mix, returned)


def tie(*values):
    return lax.optimization_barrier(values)


def local(tokens, expert_ids, route_weight, gate_up, down_proj):
    flight = lax.axis_size("ep")
    n_tp = lax.axis_size("tp")
    features = tokens.shape[1]
    cols = features // QUARTERS
    units = gate_up.shape[2] // n_tp
    pieces = units // PIECE
    up_weights = gate_up.reshape(2, n_tp * pieces, PIECE, features)
    me = lax.axis_index("tp").astype(jnp.int32).reshape(1)
    near = [(i, i ^ 1) for i in range(n_tp)]
    far = [(i, i ^ 2) for i in range(n_tp)]

    def pair_sum(got, keep):
        return (got.astype(F32) + keep.astype(F32)).astype(BF16)

    sent = pack(expert_ids.T, tokens, flight)
    sent, up_weights = tie(sent, up_weights)
    first_weights = lax.dynamic_slice_in_dim(up_weights, (me[0] ^ 3) * pieces, pieces, axis=1)
    received = lax.all_to_all(sent.reshape(flight, BLOCK, cols), "ep", 0, 0, tiled=True).reshape(flight * BLOCK, cols)

    rows, far_1, far_2 = first_part(received, first_weights)
    got_1 = lax.ppermute(far_1, "tp", near)
    got_2 = lax.ppermute(far_2, "tp", near)
    keep_1, keep_2 = parts(me, 2, rows, up_weights, 1, pieces - 1)
    pair_1 = pair_sum(got_1, keep_1)
    rows, pair_1 = tie(rows, pair_1)
    got_1 = lax.ppermute(pair_1, "tp", far)
    (for_near,) = parts(me, 1, rows, up_weights, pieces)
    got_near = lax.ppermute(for_near, "tp", near)
    for_near, got_2 = tie(for_near, got_2)
    pair_2 = pair_sum(got_2, keep_2)
    rows, pair_2, got_1 = tie(rows, pair_2, got_1)
    got_2 = lax.ppermute(pair_2, "tp", far)
    (keep,) = parts(me, 0, rows, up_weights, pieces)
    got = [got_1] + [got_2[:, p * 2 * PIECE : (p + 1) * 2 * PIECE] for p in range(pieces - 1)]
    hidden = []
    for p in range(pieces):
        columns = slice(p * 2 * PIECE, (p + 1) * 2 * PIECE)
        summed = got[p].astype(F32) + got_near[:, columns].astype(F32) + keep[:, columns].astype(F32)
        hidden.append((jax.nn.silu(summed[:, :PIECE]) * summed[:, PIECE:]).astype(BF16))
    hidden = lax.all_gather(jnp.concatenate(hidden, axis=1), "tp", axis=0, tiled=False)

    result = down(hidden, down_proj[0])
    returned = lax.all_to_all(result.reshape(flight, BLOCK, cols), "ep", 0, 0, tiled=True).reshape(flight * BLOCK, cols)
    mix = mixer(expert_ids, route_weight, flight)
    return combine(mix, returned)


def solution(mesh):
    return jax.shard_map(
        local,
        mesh=mesh,
        in_specs=(
            P(("dp", "ep"), "tp"),
            P(("dp", "ep"), None),
            P(("dp", "ep"), None),
            P("ep", None, None, "tp"),
            P("ep", None, "tp"),
        ),
        out_specs=P(("dp", "ep"), "tp"),
        check_vma=False,
    )
```

```python
import functools

import jax
import jax.numpy as jnp
import numpy as np
from jax import lax
from jax.experimental import pallas as pl
from jax.experimental.pallas import tpu as pltpu
from jax.sharding import PartitionSpec as P

CAP = 10
QUARTERS = 4
FAR = 200.0
APART = 512.0
BF16 = jnp.bfloat16
F32 = jnp.float32
PARAMS = pltpu.CompilerParams(vmem_limit_bytes=48 * 1024 * 1024)
BLOCK = QUARTERS * CAP
GROUP = 8
PIECE = 128


def mm(a, b):
    return jnp.dot(a, b, preferred_element_type=F32)


def mm_t(a, b):
    return lax.dot_general(a, b, (((1,), (1,)), ((), ())), preferred_element_type=F32)


def place_code(flight):
    rows = np.arange(flight * BLOCK)
    expert, quarter, slot = rows // BLOCK, rows // CAP % QUARTERS, rows % CAP
    code = np.zeros((rows.size, flight + 16), np.float32)
    code[rows, expert] = 1
    code[:, flight] = -slot
    code[rows, flight + 1 + quarter] = APART
    return code


def quarter_code(rows):
    code = np.zeros((16, QUARTERS * rows), np.float32)
    code[0] = 1
    for quarter in range(QUARTERS):
        code[1 + quarter] = np.arange(QUARTERS * rows) // rows != quarter
    return code


def counter(shape, dim):
    return lax.broadcasted_iota(jnp.int32, shape, dim).astype(F32)


def split(number, size):
    quotient = jnp.floor((number + 0.5) * (1.0 / size))
    return quotient, number - size * quotient


def regroup_matrix(back):
    span = GROUP * BLOCK
    row = counter((span, 1), 0)
    if back:
        source, rest = split(row, BLOCK)
        quarter, slot = split(rest, CAP)
        column = quarter * (GROUP * CAP) + source * CAP + slot
    else:
        quarter, rest = split(row, GROUP * CAP)
        source, slot = split(rest, CAP)
        column = source * BLOCK + quarter * CAP + slot
    return jnp.where(counter((span, span), 1) == column, 1.0, 0.0).astype(BF16)


def spread(rows, out_ref):
    cols = out_ref.shape[1]
    span, slab = GROUP * BLOCK, GROUP * CAP
    matrix = regroup_matrix(True)
    for g in range(out_ref.shape[0] // span):
        block = rows[g * slab : (g + 1) * slab, :]
        stacked = jnp.concatenate([block[:, q * cols : (q + 1) * cols] for q in range(QUARTERS)], axis=0)
        out_ref[g * span : (g + 1) * span, :] = mm(matrix, stacked).astype(BF16)


def pack_kernel(flight, ids_ref, token_ref, out_ref):
    top, rows = ids_ref.shape
    expert = lax.broadcasted_iota(jnp.int32, (flight, rows), 0)
    named = jnp.zeros((flight, rows), F32)
    for k in range(top):
        named += jnp.where(ids_ref[k : k + 1, :] == expert, 1.0, 0.0)
    earlier = jnp.where(counter((rows, rows), 0) < counter((rows, rows), 1), 1.0, 0.0).astype(BF16)
    slot = jnp.where(named > 0, mm(named.astype(BF16), earlier), FAR)

    ones = jnp.where(counter((16, rows), 0) == 0, 1.0, 0.0)
    code = jnp.concatenate([slot, ones], axis=0).astype(BF16)
    places = flight * CAP
    owner, place_slot = split(counter((places, 1), 0), CAP)
    column = counter((places, flight + 16), 1)
    place_code = jnp.where(column == owner, 1.0, 0.0) + jnp.where(column == flight, -place_slot, 0.0)
    gap = mm(place_code.astype(BF16), code)
    selector = jnp.where(gap == 0, 1.0, 0.0).astype(BF16)
    spread(mm(selector, token_ref[...]).astype(BF16), out_ref)


def pack(ids_t, tokens, flight):
    features = tokens.shape[1]
    whole = lambda shape: pl.BlockSpec(shape, lambda i: (0, 0))
    shape = (flight * BLOCK, features // QUARTERS)
    return pl.pallas_call(
        functools.partial(pack_kernel, flight),
        out_shape=jax.ShapeDtypeStruct(shape, BF16),
        grid=(1,),
        in_specs=[whole(ids_t.shape), whole(tokens.shape)],
        out_specs=whole(shape),
        compiler_params=pltpu.CompilerParams(vmem_limit_bytes=60 * 1024 * 1024),
        name="pack",
    )(ids_t, tokens)


def first_kernel(x_ref, weight_ref, rows_ref, first_ref, rest_ref):
    cols = x_ref.shape[1]
    span, slab = GROUP * BLOCK, GROUP * CAP
    regroup = regroup_matrix(False)
    for g in range(x_ref.shape[0] // span):
        sorted_rows = mm(regroup, x_ref[g * span : (g + 1) * span, :]).astype(BF16)
        for q in range(QUARTERS):
            rows_ref[g * slab : (g + 1) * slab, q * cols : (q + 1) * cols] = sorted_rows[q * slab : (q + 1) * slab]
    for piece in range(weight_ref.shape[1]):
        product = mm_t(rows_ref[...], weight_ref[:, piece].reshape(2 * PIECE, -1)).astype(BF16)
        if piece == 0:
            first_ref[...] = product
        else:
            rest_ref[:, (piece - 1) * 2 * PIECE : piece * 2 * PIECE] = product


def first_part(received, weights):
    places, cols = received.shape
    rows, features = places // QUARTERS, QUARTERS * cols
    pieces = weights.shape[1]
    shapes = [(rows, features), (rows, 2 * PIECE), (rows, 2 * PIECE * (pieces - 1))]
    vmem = pl.BlockSpec(memory_space=pltpu.VMEM)
    return pl.pallas_call(
        first_kernel,
        out_shape=tuple(jax.ShapeDtypeStruct(shape, BF16) for shape in shapes),
        in_specs=[vmem, vmem],
        out_specs=(vmem,) * 3,
        compiler_params=pltpu.CompilerParams(vmem_limit_bytes=24 * 1024 * 1024),
        cost_estimate=pl.CostEstimate(flops=2 * rows * weights.size, bytes_accessed=2 * weights.size, transcendentals=0),
        name="first",
    )(received, weights)


def parts_kernel(mask, me_ref, rows_ref, weight_ref, *refs):
    *out_refs, held, arrived = refs
    pieces = held.shape[1]
    base = (me_ref[0] ^ mask) * pieces
    copies = [
        pltpu.make_async_copy(weight_ref.at[:, pl.ds(base + p, 1)], held.at[:, pl.ds(p, 1)], arrived.at[p])
        for p in range(pieces)
    ]
    for copy in copies:
        copy.start()
    piece = 0
    for out_ref in out_refs:
        for p in range(out_ref.shape[1] // (2 * PIECE)):
            copies[piece].wait()
            product = mm_t(rows_ref[...], held[:, piece].reshape(2 * PIECE, -1))
            out_ref[:, p * 2 * PIECE : (p + 1) * 2 * PIECE] = product.astype(BF16)
            piece += 1


def parts(me, mask, rows_in, weights, *pieces):
    rows, features = rows_in.shape
    count = sum(pieces)
    shapes = [(rows, 2 * PIECE * number) for number in pieces]
    vmem = pl.BlockSpec(memory_space=pltpu.VMEM)
    return pl.pallas_call(
        functools.partial(parts_kernel, mask),
        out_shape=tuple(jax.ShapeDtypeStruct(shape, BF16) for shape in shapes),
        in_specs=[pl.BlockSpec(memory_space=pltpu.SMEM), vmem, pl.BlockSpec(memory_space=pl.ANY)],
        out_specs=(vmem,) * len(shapes),
        scratch_shapes=[pltpu.VMEM((2, count, PIECE, features), BF16), pltpu.SemaphoreType.DMA((count,))],
        compiler_params=PARAMS,
        cost_estimate=pl.CostEstimate(flops=4 * count * rows * PIECE * features, bytes_accessed=4 * count * PIECE * features, transcendentals=0),
        name="parts",
    )(me, rows_in, weights)


def down_kernel(hidden_ref, weight_ref, out_ref):
    hidden = jnp.concatenate([hidden_ref[k] for k in range(hidden_ref.shape[0])], axis=1)
    spread(mm(hidden, weight_ref[...]).astype(BF16), out_ref)


def down(hidden, weights):
    parts, rows, units = hidden.shape
    cols = weights.shape[1] // QUARTERS
    vmem = pl.BlockSpec(memory_space=pltpu.VMEM)
    return pl.pallas_call(
        down_kernel,
        out_shape=jax.ShapeDtypeStruct((rows * QUARTERS, cols), BF16),
        in_specs=[vmem, vmem],
        out_specs=vmem,
        compiler_params=pltpu.CompilerParams(vmem_limit_bytes=24 * 1024 * 1024),
        name="down",
    )(hidden, weights)


def mixer_kernel(ids_ref, weight_ref, earlier_ref, expert_ref, slot_ref, quarter_ref, out_ref):
    rows, top = ids_ref.shape
    flight = expert_ref.shape[0]
    expert = lax.broadcasted_iota(jnp.int32, (rows, flight), 1)
    named = jnp.zeros((rows, flight), F32)
    weight = jnp.zeros((rows, flight), F32)
    for k in range(top):
        hit = ids_ref[:, k : k + 1] == expert
        named += jnp.where(hit, 1.0, 0.0)
        weight += jnp.where(hit, weight_ref[:, k : k + 1], 0.0)
    slot = mm(earlier_ref[...], named.astype(BF16))
    slot = jnp.where(named > 0, slot, FAR).astype(BF16)
    gap = mm(slot, expert_ref[...]) + mm(quarter_ref[...], slot_ref[...])
    out_ref[...] = jnp.where(gap == 0, mm(weight.astype(BF16), expert_ref[...]), 0.0).astype(BF16)


def mixer(ids, weight, flight):
    rows = ids.shape[0]
    places = flight * BLOCK
    code = place_code(flight).T
    earlier = jnp.asarray(np.tril(np.ones((rows, rows), np.float32), -1), BF16)
    expert, slot = jnp.asarray(code[:flight], BF16), jnp.asarray(code[flight:], BF16)
    quarter = jnp.asarray(quarter_code(rows).T, BF16)
    whole = lambda a: pl.BlockSpec(a.shape, lambda i: (0, 0))
    return pl.pallas_call(
        mixer_kernel,
        out_shape=jax.ShapeDtypeStruct((QUARTERS * rows, places), BF16),
        grid=(QUARTERS,),
        in_specs=[whole(ids), whole(weight), whole(earlier), whole(expert), whole(slot),
                  pl.BlockSpec((rows, 16), lambda i: (i, 0))],
        out_specs=pl.BlockSpec((rows, places), lambda i: (i, 0)),
        compiler_params=PARAMS,
        name="mixer",
    )(ids, weight, earlier, expert, slot, quarter)


def combine_kernel(mixer_ref, returned_ref, out_ref):
    rows = out_ref.shape[0]
    cols = returned_ref.shape[1]
    for q in range(QUARTERS):
        mixed = mm(mixer_ref[q * rows : (q + 1) * rows, :], returned_ref[...])
        out_ref[:, q * cols : (q + 1) * cols] = mixed.astype(BF16)


def combine(mix, returned):
    cols = returned.shape[1]
    vmem = pl.BlockSpec(memory_space=pltpu.VMEM)
    return pl.pallas_call(
        combine_kernel,
        out_shape=jax.ShapeDtypeStruct((mix.shape[0] // QUARTERS, QUARTERS * cols), BF16),
        in_specs=[vmem, vmem],
        out_specs=vmem,
        compiler_params=pltpu.CompilerParams(vmem_limit_bytes=24 * 1024 * 1024),
        name="combine",
    )(mix, returned)


def tie(*values):
    return lax.optimization_barrier(values)


def local(tokens, expert_ids, route_weight, gate_up, down_proj):
    flight = lax.axis_size("ep")
    n_tp = lax.axis_size("tp")
    features = tokens.shape[1]
    cols = features // QUARTERS
    units = gate_up.shape[2] // n_tp
    pieces = units // PIECE
    up_weights = gate_up.reshape(2, n_tp * pieces, PIECE, features)
    me = lax.axis_index("tp").astype(jnp.int32).reshape(1)
    near = [(i, i ^ 1) for i in range(n_tp)]
    far = [(i, i ^ 2) for i in range(n_tp)]

    def pair_sum(got, keep):
        return (got.astype(F32) + keep.astype(F32)).astype(BF16)

    sent = pack(expert_ids.T, tokens, flight)
    sent, up_weights = tie(sent, up_weights)
    first_weights = lax.dynamic_slice_in_dim(up_weights, (me[0] ^ 3) * pieces, pieces, axis=1)
    received = lax.all_to_all(sent.reshape(flight, BLOCK, cols), "ep", 0, 0, tiled=True).reshape(flight * BLOCK, cols)

    rows, far_1, far_2 = first_part(received, first_weights)
    got_1 = lax.ppermute(far_1, "tp", near)
    keep_1, keep_2 = parts(me, 2, rows, up_weights, 1, pieces - 1)
    far_2, keep_1 = tie(far_2, keep_1)
    got_2 = lax.ppermute(far_2, "tp", near)
    pair_1 = pair_sum(got_1, keep_1)
    rows, pair_1 = tie(rows, pair_1)
    got_1 = lax.ppermute(pair_1, "tp", far)
    (for_near,) = parts(me, 1, rows, up_weights, pieces)
    got_near = lax.ppermute(for_near, "tp", near)
    for_near, got_2 = tie(for_near, got_2)
    pair_2 = pair_sum(got_2, keep_2)
    rows, pair_2, got_1 = tie(rows, pair_2, got_1)
    got_2 = lax.ppermute(pair_2, "tp", far)
    (keep,) = parts(me, 0, rows, up_weights, pieces)
    got = [got_1] + [got_2[:, p * 2 * PIECE : (p + 1) * 2 * PIECE] for p in range(pieces - 1)]
    hidden = []
    for p in range(pieces):
        columns = slice(p * 2 * PIECE, (p + 1) * 2 * PIECE)
        summed = got[p].astype(F32) + got_near[:, columns].astype(F32) + keep[:, columns].astype(F32)
        hidden.append((jax.nn.silu(summed[:, :PIECE]) * summed[:, PIECE:]).astype(BF16))
    hidden = lax.all_gather(jnp.concatenate(hidden, axis=1), "tp", axis=0, tiled=False)

    result = down(hidden, down_proj[0])
    returned = lax.all_to_all(result.reshape(flight, BLOCK, cols), "ep", 0, 0, tiled=True).reshape(flight * BLOCK, cols)
    mix = mixer(expert_ids, route_weight, flight)
    return combine(mix, returned)


def solution(mesh):
    return jax.shard_map(
        local,
        mesh=mesh,
        in_specs=(
            P(("dp", "ep"), "tp"),
            P(("dp", "ep"), None),
            P(("dp", "ep"), None),
            P("ep", None, None, "tp"),
            P("ep", None, "tp"),
        ),
        out_specs=P(("dp", "ep"), "tp"),
        check_vma=False,
    )
```

```python
import functools

import jax
import jax.numpy as jnp
import numpy as np
from jax import lax
from jax.experimental import pallas as pl
from jax.experimental.pallas import tpu as pltpu
from jax.sharding import PartitionSpec as P

CAP = 10
QUARTERS = 4
FAR = 200.0
APART = 512.0
BF16 = jnp.bfloat16
F32 = jnp.float32
PARAMS = pltpu.CompilerParams(vmem_limit_bytes=48 * 1024 * 1024)
BLOCK = QUARTERS * CAP
GROUP = 8
PIECE = 128


def mm(a, b):
    return jnp.dot(a, b, preferred_element_type=F32)


def mm_t(a, b):
    return lax.dot_general(a, b, (((1,), (1,)), ((), ())), preferred_element_type=F32)


def place_code(flight):
    rows = np.arange(flight * BLOCK)
    expert, quarter, slot = rows // BLOCK, rows // CAP % QUARTERS, rows % CAP
    code = np.zeros((rows.size, flight + 16), np.float32)
    code[rows, expert] = 1
    code[:, flight] = -slot
    code[rows, flight + 1 + quarter] = APART
    return code


def quarter_code(rows):
    code = np.zeros((16, QUARTERS * rows), np.float32)
    code[0] = 1
    for quarter in range(QUARTERS):
        code[1 + quarter] = np.arange(QUARTERS * rows) // rows != quarter
    return code


def counter(shape, dim):
    return lax.broadcasted_iota(jnp.int32, shape, dim).astype(F32)


def split(number, size):
    quotient = jnp.floor((number + 0.5) * (1.0 / size))
    return quotient, number - size * quotient


def regroup_matrix(back):
    span = GROUP * BLOCK
    row = counter((span, 1), 0)
    if back:
        source, rest = split(row, BLOCK)
        quarter, slot = split(rest, CAP)
        column = quarter * (GROUP * CAP) + source * CAP + slot
    else:
        quarter, rest = split(row, GROUP * CAP)
        source, slot = split(rest, CAP)
        column = source * BLOCK + quarter * CAP + slot
    return jnp.where(counter((span, span), 1) == column, 1.0, 0.0).astype(BF16)


def spread(rows, out_ref):
    cols = out_ref.shape[1]
    span, slab = GROUP * BLOCK, GROUP * CAP
    matrix = regroup_matrix(True)
    for g in range(out_ref.shape[0] // span):
        block = rows[g * slab : (g + 1) * slab, :]
        stacked = jnp.concatenate([block[:, q * cols : (q + 1) * cols] for q in range(QUARTERS)], axis=0)
        out_ref[g * span : (g + 1) * span, :] = mm(matrix, stacked).astype(BF16)


def pack_kernel(flight, ids_ref, token_ref, out_ref):
    top, rows = ids_ref.shape
    expert = lax.broadcasted_iota(jnp.int32, (flight, rows), 0)
    named = jnp.zeros((flight, rows), F32)
    for k in range(top):
        named += jnp.where(ids_ref[k : k + 1, :] == expert, 1.0, 0.0)
    earlier = jnp.where(counter((rows, rows), 0) < counter((rows, rows), 1), 1.0, 0.0).astype(BF16)
    slot = jnp.where(named > 0, mm(named.astype(BF16), earlier), FAR)

    ones = jnp.where(counter((16, rows), 0) == 0, 1.0, 0.0)
    code = jnp.concatenate([slot, ones], axis=0).astype(BF16)
    places = flight * CAP
    owner, place_slot = split(counter((places, 1), 0), CAP)
    column = counter((places, flight + 16), 1)
    place_code = jnp.where(column == owner, 1.0, 0.0) + jnp.where(column == flight, -place_slot, 0.0)
    gap = mm(place_code.astype(BF16), code)
    selector = jnp.where(gap == 0, 1.0, 0.0).astype(BF16)
    spread(mm(selector, token_ref[...]).astype(BF16), out_ref)


def pack(ids_t, tokens, flight):
    features = tokens.shape[1]
    whole = lambda shape: pl.BlockSpec(shape, lambda i: (0, 0))
    shape = (flight * BLOCK, features // QUARTERS)
    return pl.pallas_call(
        functools.partial(pack_kernel, flight),
        out_shape=jax.ShapeDtypeStruct(shape, BF16),
        grid=(1,),
        in_specs=[whole(ids_t.shape), whole(tokens.shape)],
        out_specs=whole(shape),
        compiler_params=pltpu.CompilerParams(vmem_limit_bytes=60 * 1024 * 1024),
        name="pack",
    )(ids_t, tokens)


def first_kernel(x_ref, weight_ref, rows_ref, first_ref, rest_ref):
    cols = x_ref.shape[1]
    span, slab = GROUP * BLOCK, GROUP * CAP
    regroup = regroup_matrix(False)
    for g in range(x_ref.shape[0] // span):
        sorted_rows = mm(regroup, x_ref[g * span : (g + 1) * span, :]).astype(BF16)
        for q in range(QUARTERS):
            rows_ref[g * slab : (g + 1) * slab, q * cols : (q + 1) * cols] = sorted_rows[q * slab : (q + 1) * slab]
    for piece in range(weight_ref.shape[1]):
        product = mm_t(rows_ref[...], weight_ref[:, piece].reshape(2 * PIECE, -1)).astype(BF16)
        if piece == 0:
            first_ref[...] = product
        else:
            rest_ref[:, (piece - 1) * 2 * PIECE : piece * 2 * PIECE] = product


def first_part(received, weights):
    places, cols = received.shape
    rows, features = places // QUARTERS, QUARTERS * cols
    pieces = weights.shape[1]
    shapes = [(rows, features), (rows, 2 * PIECE), (rows, 2 * PIECE * (pieces - 1))]
    vmem = pl.BlockSpec(memory_space=pltpu.VMEM)
    return pl.pallas_call(
        first_kernel,
        out_shape=tuple(jax.ShapeDtypeStruct(shape, BF16) for shape in shapes),
        in_specs=[vmem, vmem],
        out_specs=(vmem,) * 3,
        compiler_params=pltpu.CompilerParams(vmem_limit_bytes=24 * 1024 * 1024),
        cost_estimate=pl.CostEstimate(flops=2 * rows * weights.size, bytes_accessed=2 * weights.size, transcendentals=0),
        name="first",
    )(received, weights)


def parts_kernel(mask, me_ref, rows_ref, weight_ref, *refs):
    *out_refs, held, arrived = refs
    pieces = held.shape[1]
    base = (me_ref[0] ^ mask) * pieces
    copies = [
        pltpu.make_async_copy(weight_ref.at[:, pl.ds(base + p, 1)], held.at[:, pl.ds(p, 1)], arrived.at[p])
        for p in range(pieces)
    ]
    for copy in copies:
        copy.start()
    piece = 0
    for out_ref in out_refs:
        for p in range(out_ref.shape[1] // (2 * PIECE)):
            copies[piece].wait()
            product = mm_t(rows_ref[...], held[:, piece].reshape(2 * PIECE, -1))
            out_ref[:, p * 2 * PIECE : (p + 1) * 2 * PIECE] = product.astype(BF16)
            piece += 1


def parts(me, mask, rows_in, weights, *pieces):
    rows, features = rows_in.shape
    count = sum(pieces)
    shapes = [(rows, 2 * PIECE * number) for number in pieces]
    vmem = pl.BlockSpec(memory_space=pltpu.VMEM)
    return pl.pallas_call(
        functools.partial(parts_kernel, mask),
        out_shape=tuple(jax.ShapeDtypeStruct(shape, BF16) for shape in shapes),
        in_specs=[pl.BlockSpec(memory_space=pltpu.SMEM), vmem, pl.BlockSpec(memory_space=pl.ANY)],
        out_specs=(vmem,) * len(shapes),
        scratch_shapes=[pltpu.VMEM((2, count, PIECE, features), BF16), pltpu.SemaphoreType.DMA((count,))],
        compiler_params=PARAMS,
        cost_estimate=pl.CostEstimate(flops=4 * count * rows * PIECE * features, bytes_accessed=4 * count * PIECE * features, transcendentals=0),
        name="parts",
    )(me, rows_in, weights)


def down_kernel(hidden_ref, weight_ref, out_ref):
    hidden = jnp.concatenate([hidden_ref[k] for k in range(hidden_ref.shape[0])], axis=1)
    spread(mm(hidden, weight_ref[...]).astype(BF16), out_ref)


def down(hidden, weights):
    parts, rows, units = hidden.shape
    cols = weights.shape[1] // QUARTERS
    vmem = pl.BlockSpec(memory_space=pltpu.VMEM)
    return pl.pallas_call(
        down_kernel,
        out_shape=jax.ShapeDtypeStruct((rows * QUARTERS, cols), BF16),
        in_specs=[vmem, vmem],
        out_specs=vmem,
        compiler_params=pltpu.CompilerParams(vmem_limit_bytes=24 * 1024 * 1024),
        name="down",
    )(hidden, weights)


def mixer_kernel(ids_ref, weight_ref, earlier_ref, expert_ref, slot_ref, quarter_ref, out_ref):
    rows, top = ids_ref.shape
    flight = expert_ref.shape[0]
    expert = lax.broadcasted_iota(jnp.int32, (rows, flight), 1)
    named = jnp.zeros((rows, flight), F32)
    weight = jnp.zeros((rows, flight), F32)
    for k in range(top):
        hit = ids_ref[:, k : k + 1] == expert
        named += jnp.where(hit, 1.0, 0.0)
        weight += jnp.where(hit, weight_ref[:, k : k + 1], 0.0)
    slot = mm(earlier_ref[...], named.astype(BF16))
    slot = jnp.where(named > 0, slot, FAR).astype(BF16)
    gap = mm(slot, expert_ref[...]) + mm(quarter_ref[...], slot_ref[...])
    out_ref[...] = jnp.where(gap == 0, mm(weight.astype(BF16), expert_ref[...]), 0.0).astype(BF16)


def mixer(ids, weight, flight):
    rows = ids.shape[0]
    places = flight * BLOCK
    code = place_code(flight).T
    earlier = jnp.asarray(np.tril(np.ones((rows, rows), np.float32), -1), BF16)
    expert, slot = jnp.asarray(code[:flight], BF16), jnp.asarray(code[flight:], BF16)
    quarter = jnp.asarray(quarter_code(rows).T, BF16)
    whole = lambda a: pl.BlockSpec(a.shape, lambda i: (0, 0))
    return pl.pallas_call(
        mixer_kernel,
        out_shape=jax.ShapeDtypeStruct((QUARTERS * rows, places), BF16),
        grid=(QUARTERS,),
        in_specs=[whole(ids), whole(weight), whole(earlier), whole(expert), whole(slot),
                  pl.BlockSpec((rows, 16), lambda i: (i, 0))],
        out_specs=pl.BlockSpec((rows, places), lambda i: (i, 0)),
        compiler_params=PARAMS,
        name="mixer",
    )(ids, weight, earlier, expert, slot, quarter)


def combine_kernel(mixer_ref, returned_ref, out_ref):
    rows = out_ref.shape[0]
    cols = returned_ref.shape[1]
    for q in range(QUARTERS):
        mixed = mm(mixer_ref[q * rows : (q + 1) * rows, :], returned_ref[...])
        out_ref[:, q * cols : (q + 1) * cols] = mixed.astype(BF16)


def combine(mix, returned):
    cols = returned.shape[1]
    vmem = pl.BlockSpec(memory_space=pltpu.VMEM)
    return pl.pallas_call(
        combine_kernel,
        out_shape=jax.ShapeDtypeStruct((mix.shape[0] // QUARTERS, QUARTERS * cols), BF16),
        in_specs=[vmem, vmem],
        out_specs=vmem,
        compiler_params=pltpu.CompilerParams(vmem_limit_bytes=24 * 1024 * 1024),
        name="combine",
    )(mix, returned)


def tie(*values):
    return lax.optimization_barrier(values)


def local(tokens, expert_ids, route_weight, gate_up, down_proj):
    flight = lax.axis_size("ep")
    n_tp = lax.axis_size("tp")
    features = tokens.shape[1]
    cols = features // QUARTERS
    units = gate_up.shape[2] // n_tp
    pieces = units // PIECE
    up_weights = gate_up.reshape(2, n_tp * pieces, PIECE, features)
    me = lax.axis_index("tp").astype(jnp.int32).reshape(1)
    near = [(i, i ^ 1) for i in range(n_tp)]
    far = [(i, i ^ 2) for i in range(n_tp)]

    def pair_sum(got, keep):
        return (got.astype(F32) + keep.astype(F32)).astype(BF16)

    sent = pack(expert_ids.T, tokens, flight)
    sent, up_weights, ids, weight = tie(sent, up_weights, expert_ids, route_weight)
    mix = mixer(ids, weight, flight)
    first_weights = lax.dynamic_slice_in_dim(up_weights, (me[0] ^ 3) * pieces, pieces, axis=1)
    received = lax.all_to_all(sent.reshape(flight, BLOCK, cols), "ep", 0, 0, tiled=True).reshape(flight * BLOCK, cols)

    received, mix = tie(received, mix)
    rows, far_1, far_2 = first_part(received, first_weights)
    got_1 = lax.ppermute(far_1, "tp", near)
    got_2 = lax.ppermute(far_2, "tp", near)
    keep_1, keep_2 = parts(me, 2, rows, up_weights, 1, pieces - 1)
    pair_1 = pair_sum(got_1, keep_1)
    rows, pair_1 = tie(rows, pair_1)
    got_1 = lax.ppermute(pair_1, "tp", far)
    (for_near,) = parts(me, 1, rows, up_weights, pieces)
    got_near = lax.ppermute(for_near, "tp", near)
    for_near, got_2 = tie(for_near, got_2)
    pair_2 = pair_sum(got_2, keep_2)
    rows, pair_2, got_1 = tie(rows, pair_2, got_1)
    got_2 = lax.ppermute(pair_2, "tp", far)
    (keep,) = parts(me, 0, rows, up_weights, pieces)
    got = [got_1] + [got_2[:, p * 2 * PIECE : (p + 1) * 2 * PIECE] for p in range(pieces - 1)]
    hidden = []
    for p in range(pieces):
        columns = slice(p * 2 * PIECE, (p + 1) * 2 * PIECE)
        summed = got[p].astype(F32) + got_near[:, columns].astype(F32) + keep[:, columns].astype(F32)
        hidden.append((jax.nn.silu(summed[:, :PIECE]) * summed[:, PIECE:]).astype(BF16))
    hidden = lax.all_gather(jnp.concatenate(hidden, axis=1), "tp", axis=0, tiled=False)

    result = down(hidden, down_proj[0])
    returned = lax.all_to_all(result.reshape(flight, BLOCK, cols), "ep", 0, 0, tiled=True).reshape(flight * BLOCK, cols)
    return combine(mix, returned)


def solution(mesh):
    return jax.shard_map(
        local,
        mesh=mesh,
        in_specs=(
            P(("dp", "ep"), "tp"),
            P(("dp", "ep"), None),
            P(("dp", "ep"), None),
            P("ep", None, None, "tp"),
            P("ep", None, "tp"),
        ),
        out_specs=P(("dp", "ep"), "tp"),
        check_vma=False,
    )
```
